32 devices in a mesh: dp: 8 (over z, x), ctx: 4 (over y, core).
Axes of the slice: x: 2, y: 2, z: 4, core: 2. Of those that a mesh axis runs over, the one named last changes fastest.
Arguments:
- tokens: bfloat16 [16, 1024, 768], P('dp', 'ctx'), may hold values from -6 to 6
- norm_weight: bfloat16 [768], P('dp'), may hold values from 0.5 to 1.5
- in_weight: bfloat16 [768, 3352], P('dp'), may hold values from -0.21875 to 0.21875
- conv_weight: bfloat16 [4, 1792], P(None, 'dp'), may hold values from -3 to 3
- conv_bias: bfloat16 [1792], P('dp'), may hold values from -3 to 3
- decay_log: float32 [24], replicated, may hold values from 0 to 2.77
- skip_gain: float32 [24], replicated, may hold values from 0.5 to 1.5
- step_bias: float32 [24], replicated, may hold values from -7 to -3
- gated_gain: bfloat16 [1536], P('dp'), may hold values from 0.5 to 1.5
- out_weight: bfloat16 [1536, 768], P('dp'), may hold values from -0.15625 to 0.15625
- cotangent: bfloat16 [16, 1024, 768], P('dp', 'ctx'), may hold values from -6 to 6
Outputs:
- block_output: bfloat16 [16, 1024, 768], P('dp', 'ctx')
- input_grad: bfloat16 [16, 1024, 768], P('dp', 'ctx')
- norm_grad: float32 [768], P('dp')
- in_grad: float32 [768, 3352], P('dp')
- conv_grad: float32 [4, 1792], P(None, 'dp')
- conv_bias_grad: float32 [1792], P('dp')
- decay_log_grad: float32 [24], replicated
- skip_grad: float32 [24], replicated
- step_bias_grad: float32 [24], replicated
- gated_grad: float32 [1536], P('dp')
- out_grad: float32 [1536, 768], P('dp')
The draws below stay inside these ranges and needn't reach their ends.
All inputs are finite; a program needn't handle non-finite values.
Results may differ from the reference program's by a relative error of at most 0.0091.
Values may be sent and summed in bfloat16 or wider, within the bound.
A program may use at most 192 MiB of HBM per device.

```python
import math
import jax
import jax.numpy as jnp
from jax import lax

D = 768
HEADS = 24
HEADDIM = 64
NSTATE = 128
CONV = 4
SPAN = 128
INNER = 1536
XBC = 1792
PROJ = 3352
SEQS = 16
LEN = 1024


def raised(values, own_key, source, target, blocks, factor):
    owner, partner = [(jnp.arange(values.shape[axis_at]) // (values.shape[axis_at] // blocks)).reshape([-1 if axis == axis_at else 1 for axis in range(values.ndim)]) for axis_at in (source, target)]
    chosen = jax.random.permutation(own_key, blocks)[partner]
    strong = (owner == chosen) | (owner == (partner + blocks // 2) % blocks)
    return jnp.where(strong, factor * values, values)


def block_levels(rng, shape, split, smallest, high):
    factor_of, own = 1.0, jax.random.fold_in(rng, 6)
    for axis_at, parts in split:
        heights = jnp.exp(jax.random.uniform(jax.random.fold_in(own, axis_at), (parts,), jnp.float32, smallest / len(split), high / len(split)))
        factor_of = factor_of * jnp.repeat(heights, shape[axis_at] // parts).reshape([-1 if axis == axis_at else 1 for axis in range(len(shape))])
    return factor_of


def centred(stream_key, extent, width, reach, cuts=(), kind=jnp.bfloat16):
    level = block_levels(stream_key, extent, cuts, -0.22, 0.18) if cuts else 1.0
    drawn = jax.random.normal(stream_key, extent, jnp.float32) * width * level
    return jnp.minimum(jnp.maximum(drawn, -reach), reach).astype(kind)


def heavy_noise(own_key, dims, width, bound, cuts, heavy, held_as=jnp.bfloat16):
    values = width * jax.random.normal(own_key, dims, jnp.float32)
    if cuts:
        values = values * block_levels(own_key, dims, cuts, -0.22, 0.18)
    return jnp.clip(raised(values, jax.random.fold_in(own_key, 3), *heavy), -bound, bound).astype(held_as)


def setup_inputs(seed: int = 0) -> dict:
    seeds = jax.random.split(jax.random.key(seed), 12)
    return {
        "tokens": heavy_noise(seeds[0], (SEQS, LEN, D), 1.0, 6.0, ((0, 8), (1, 4)), (0, 2, 8, 2.0)),
        "norm_weight": jnp.clip(1.0 + 0.1 * jax.random.normal(seeds[1], (D,), jnp.float32), 0.5, 1.5).astype(jnp.bfloat16),
        "in_weight": centred(seeds[2], (D, PROJ), D ** -0.5, 0.21875, ((0, 8),)),
        "conv_weight": centred(seeds[3], (CONV, XBC), CONV ** -0.5, 3.0, ((1, 8),)),
        "conv_bias": centred(seeds[4], (XBC,), 0.5, 3.0, ((0, 8),)),
        "decay_log": jnp.clip(jax.random.uniform(seeds[5], (HEADS,), jnp.float32, 0.0, 2.77), 0.0, 2.77),
        "skip_gain": jnp.clip(jax.random.uniform(seeds[6], (HEADS,), jnp.float32, 0.5, 1.5), 0.5, 1.5),
        "step_bias": jnp.clip(jax.random.uniform(seeds[7], (HEADS,), jnp.float32, -7.0, -3.0), -7.0, -3.0),
        "gated_gain": jnp.clip(1.0 + 0.1 * jax.random.normal(seeds[8], (INNER,), jnp.float32), 0.5, 1.5).astype(jnp.bfloat16),
        "out_weight": centred(seeds[9], (INNER, D), INNER ** -0.5, 0.15625, ((0, 8),)),
        "cotangent": centred(seeds[10], (SEQS, LEN, D), 1.0, 6.0, ((0, 8), (1, 4))),
    }


epsilon = 1e-05
highest = lax.Precision.HIGHEST

@jax.custom_vjp
def low(v):
    return lax.optimization_barrier(v.astype(jnp.bfloat16)).astype(jnp.float32)

@jax.custom_vjp
def low_back(v):
    return v

def low_keep(v):
    return (low(v), None)

def low_pass(kept, grad):
    return (grad,)

def back_keep(v):
    return (v, None)

def back_low(kept, grad):
    return (low(grad),)
low.defvjp(low_keep, low_pass)
low_back.defvjp(back_keep, back_low)

def span_body(state, pieces):
    values, inputs_b, readout, log_step, step_size = pieces
    cumul = jnp.cumsum(log_step, axis=1)
    causal = jnp.tril(jnp.ones((SPAN, SPAN), jnp.bool_))
    gap = cumul[:, :, None, :] - cumul[:, None, :, :]
    decay_mat = jnp.exp(jnp.where(causal[None, :, :, None], gap, -1e+30))
    scores = jnp.einsum('btn,bsn->bts', readout, inputs_b, precision=highest)
    weights = scores[..., None] * decay_mat * step_size[:, None, :, :]
    intra_out = jnp.einsum('btsh,bshp->bthp', weights, values, precision=highest)
    inter_out = jnp.exp(cumul)[..., None] * jnp.einsum('btn,bhpn->bthp', readout, state, precision=highest)
    tail_w = jnp.exp(cumul[:, -1:, :] - cumul) * step_size
    update = jnp.einsum('bshp,bsn->bhpn', tail_w[..., None] * values, inputs_b, precision=highest)
    state = jnp.exp(cumul[:, -1, :])[..., None, None] * state + update
    return (state, intra_out + inter_out)

def scan_spans(values, inputs_b, readout, log_step, step_size):
    seq_count, length = step_size.shape[:2]
    span_count = length // SPAN

    def split_up(array):
        return jnp.moveaxis(array.reshape((seq_count, span_count, SPAN) + array.shape[2:]), 1, 0)
    zero_state = jnp.zeros((seq_count, HEADS, HEADDIM, NSTATE), jnp.float32)
    members = tuple((split_up(member) for member in (values, inputs_b, readout, log_step, step_size)))
    last_state, outputs = lax.scan(jax.checkpoint(span_body), zero_state, members)
    return jnp.moveaxis(outputs, 0, 1).reshape(seq_count, length, HEADS, HEADDIM)

def mamba_layer(stream, norm_weight, in_weight, conv_weight, conv_bias, decay_log, skip_gain, step_bias, gated_gain, out_weight):
    seq_count, length, _ = stream.shape
    inv_rms = lax.rsqrt(lax.optimization_barrier(jnp.mean(stream * stream, axis=-1, keepdims=True)) + epsilon)
    normed = low(stream * inv_rms * norm_weight)
    projected = jnp.einsum('bld,dk->blk', normed, in_weight, precision=highest)
    projected = low_back(low(projected))
    gate_raw = projected[..., :INNER]
    conv_in = projected[..., INNER:INNER + XBC]
    step_raw = projected[..., INNER + XBC:]
    padded = jnp.pad(conv_in, ((0, 0), (CONV - 1, 0), (0, 0)))
    conv_pre = conv_bias + sum((padded[:, offset:offset + length] * conv_weight[offset] for offset in range(CONV)))
    active = jax.nn.silu(conv_pre)
    values = active[..., :INNER].reshape(seq_count, length, HEADS, HEADDIM)
    inputs_b = active[..., INNER:INNER + NSTATE]
    readout = active[..., INNER + NSTATE:]
    step_size = jax.nn.softplus(step_raw + step_bias)
    rate_head = -jnp.exp(decay_log)
    ssd_out = scan_spans(values, inputs_b, readout, step_size * rate_head, step_size)
    mixed_out = (ssd_out + skip_gain[:, None] * values).reshape(seq_count, length, INNER)
    gate_val = mixed_out * jax.nn.silu(gate_raw)
    gate_rms = lax.rsqrt(lax.optimization_barrier(jnp.mean(gate_val * gate_val, axis=-1, keepdims=True)) + epsilon)
    gated = low(gate_val * gate_rms * gated_gain)
    return stream + jnp.einsum('blk,kd->bld', gated, out_weight, precision=highest)

def reference(tokens, norm_weight, in_weight, conv_weight, conv_bias, decay_log, skip_gain, step_bias, gated_gain, out_weight, cotangent):
    weights = tuple((member.astype(jnp.float32) for member in (norm_weight, in_weight, conv_weight, conv_bias, decay_log, skip_gain, step_bias, gated_gain, out_weight)))
    seq_group = math.gcd(SEQS, max(1, 4096 // LEN))
    blocks = SEQS // seq_group
    streams = tokens.astype(jnp.float32).reshape(blocks, seq_group, LEN, D)
    cotangents = cotangent.astype(jnp.float32).reshape(blocks, seq_group, LEN, D)

    def one_block(totals, pair):
        outputs, pullback = jax.vjp(mamba_layer, pair[0], *weights)
        all_grads = pullback(pair[1])
        totals = tuple((running + addend for running, addend in zip(totals, all_grads[1:])))
        return (totals, (outputs.astype(jnp.bfloat16), all_grads[0].astype(jnp.bfloat16)))
    zeros = tuple((jnp.zeros(member.shape, jnp.float32) for member in weights))
    totals, (outputs, input_grads) = lax.scan(one_block, zeros, (streams, cotangents))
    return (outputs.reshape(SEQS, LEN, D), input_grads.reshape(SEQS, LEN, D), totals[0], totals[1], totals[2], totals[3], totals[4], totals[5], totals[6], totals[7], totals[8])
```

```python
import jax
import jax.numpy as jnp
from jax import lax
from jax.experimental import pallas as pl
from jax.experimental.pallas import tpu as pltpu
from jax.sharding import PartitionSpec as P

HEADS = 24
HEADDIM = 64
NSTATE = 128
CONV = 4
SPAN = 128
INNER = 1536
XBC = 1792
WIDE = 1920
SPARE = 104
PAIRS = HEADS // 2
TAIL_ROWS = 16

epsilon = 1e-05
low = jnp.bfloat16
f32 = jnp.float32


def nn(a, b, precision=None):
    return lax.dot_general(
        a, b, (((1,), (0,)), ((), ())), precision=precision, preferred_element_type=f32
    )


def nt(a, b):
    return lax.dot_general(a, b, (((1,), (1,)), ((), ())), preferred_element_type=f32)


def tn(a, b):
    return lax.dot_general(a, b, (((0,), (0,)), ((), ())), preferred_element_type=f32)


def silu_grad(pre):
    sigma = jax.nn.sigmoid(pre)
    return sigma * (1.0 + pre * (1.0 - sigma))


def first_half(rows):
    return lax.broadcasted_iota(jnp.int32, (rows, SPAN), 1) < HEADDIM


def expand(per_head):
    rows = per_head.shape[0]
    mask = first_half(rows)
    pieces = []
    for pair in range(PAIRS):
        left = jnp.broadcast_to(per_head[:, 2 * pair : 2 * pair + 1], (rows, SPAN))
        right = jnp.broadcast_to(per_head[:, 2 * pair + 1 : 2 * pair + 2], (rows, SPAN))
        pieces.append(jnp.where(mask, left, right))
    return jnp.concatenate(pieces, axis=1)


def head_sum(wide, fold):
    high = wide.astype(low)
    rest = (wide - high.astype(f32)).astype(low)
    return nn(high, fold) + nn(rest, fold)


def diagonal(block, mask):
    zero = jnp.zeros_like(block)
    return jnp.concatenate(
        [jnp.where(mask, block, zero), jnp.where(mask, zero, block)], axis=0
    ).astype(low)


def causal_mask():
    row = lax.broadcasted_iota(jnp.int32, (SPAN, SPAN), 0)
    column = lax.broadcasted_iota(jnp.int32, (SPAN, SPAN), 1)
    return row >= column


def decay_of(cumul, cumul_t, head, causal):
    gap = cumul[:, head : head + 1] - cumul_t[head : head + 1, :]
    return jnp.exp(jnp.where(causal, gap, -1e30))


def prepare_kernel(
    cs_ref, halo_ref, taps_ref, bias_ref, head_ref,
    pre_ref, cumul_ref, cumul_t_ref, step_ref, step_t_ref, sigma_ref, update_ref, decay_ref,
    padded,
):
    padded[0:8, :] = halo_ref[0]
    padded[8:, :] = cs_ref[:, :XBC].astype(f32)
    pre = bias_ref[...] + sum(
        padded[5 + k : 5 + k + SPAN, :] * taps_ref[k : k + 1, :] for k in range(CONV)
    )
    pre_ref[...] = pre
    active = pre * jax.nn.sigmoid(pre)
    values = active[:, :INNER]
    inputs_b = active[:, INNER : INNER + NSTATE].astype(low)
    lane = lax.broadcasted_iota(jnp.int32, (SPAN, SPAN), 1)
    raw = jnp.where(lane < HEADS, cs_ref[:, XBC:].astype(f32) + head_ref[0:1, :], 0.0)
    step = jnp.maximum(raw, 0.0) + jnp.log1p(jnp.exp(-jnp.abs(raw)))
    step = jnp.where(lane < HEADS, step, 0.0)
    sigma_ref[...] = jax.nn.sigmoid(raw)
    log_step = step * (-jnp.exp(head_ref[1:2, :]))
    lower = causal_mask().astype(f32)
    cumul = nn(lower, log_step, lax.Precision.HIGHEST)
    cumul_ref[...] = cumul
    step_ref[...] = step
    cumul_t_ref[...] = cumul.T
    step_t_ref[...] = step.T
    last = cumul[SPAN - 1 : SPAN, :]
    tail = jnp.exp(last - cumul) * step
    update_ref[0] = tn(inputs_b, (expand(tail) * values).astype(low))
    decay_ref[0] = jnp.broadcast_to(expand(jnp.exp(last)), (8, INNER))


def intra_kernel(pre_ref, cumul_ref, cumul_t_ref, step_t_ref, skip_ref, out_ref):
    pre = pre_ref[...]
    active = pre * jax.nn.sigmoid(pre)
    inputs_b = active[:, INNER : INNER + NSTATE].astype(low)
    readout = active[:, INNER + NSTATE :].astype(low)
    scores = nt(readout, inputs_b)
    causal = causal_mask()
    mask = first_half(SPAN)
    cumul, cumul_t, step_t = cumul_ref[...], cumul_t_ref[...], step_t_ref[...]
    for pair in range(PAIRS):
        cut = slice(pair * SPAN, (pair + 1) * SPAN)
        values = active[:, cut]
        weights = [
            (scores * decay_of(cumul, cumul_t, h, causal) * step_t[h : h + 1, :]).astype(low)
            for h in (2 * pair, 2 * pair + 1)
        ]
        inner = nn(jnp.concatenate(weights, axis=1), diagonal(values, mask))
        out_ref[:, cut] = inner + skip_ref[:, cut] * values


def gate_kernel(
    partial_ref, pre_ref, cumul_ref, start_ref, gate_ref, dgated_ref, gain_ref, fold_ref,
    gated_ref, dgate_ref, dmixed_ref, dstart_ref, dcumul_ref, sums_ref,
):
    @pl.when((pl.program_id(0) == 0) & (pl.program_id(1) == 0))
    def _():
        sums_ref[...] = jnp.zeros_like(sums_ref)

    pre = pre_ref[...]
    active = pre * jax.nn.sigmoid(pre)
    values = active[:, :INNER]
    readout = active[:, INNER + NSTATE :].astype(low)
    growth = expand(jnp.exp(cumul_ref[...]))
    inter = growth * nn(readout, start_ref[0].astype(low))
    mixed = partial_ref[...] + inter
    gate = gate_ref[...].astype(f32)
    sigma = jax.nn.sigmoid(gate)
    act = gate * sigma
    gate_val = mixed * act
    rms = lax.rsqrt(jnp.mean(gate_val * gate_val, axis=1, keepdims=True) + epsilon)
    hat = gate_val * rms
    gain = gain_ref[...]
    gated_ref[...] = (hat * gain).astype(low)
    d_gated = dgated_ref[...]
    sums_ref[0:1, :] += jnp.sum(d_gated * hat, axis=0, keepdims=True)
    d_hat = d_gated * gain
    d_gate = rms * d_hat - hat * (rms * rms * jnp.mean(d_hat * gate_val, axis=1, keepdims=True))
    dgate_ref[...] = (d_gate * mixed * (sigma * (1.0 + gate * (1.0 - sigma)))).astype(low)
    d_mixed = d_gate * act
    dmixed_ref[...] = d_mixed
    sums_ref[1:2, :] += jnp.sum(d_mixed * values, axis=0, keepdims=True)
    dstart_ref[0] = tn(readout, (growth * d_mixed).astype(low))
    dcumul_ref[...] = head_sum(d_mixed * inter, fold_ref[...])


def local_kernel(
    pre_ref, cumul_ref, cumul_t_ref, step_ref, step_t_ref, dmixed_ref, skip_ref,
    dvalues_ref, dstep_ref, dcumul_ref, dbc_ref, rows,
):
    pre = pre_ref[...]
    active = pre * jax.nn.sigmoid(pre)
    inputs_b = active[:, INNER : INNER + NSTATE].astype(low)
    readout = active[:, INNER + NSTATE :].astype(low)
    scores = nt(readout, inputs_b)
    causal = causal_mask()
    mask = first_half(SPAN)
    lane = lax.broadcasted_iota(jnp.int32, (SPAN, SPAN), 1)
    cumul, cumul_t, step_t = cumul_ref[...], cumul_t_ref[...], step_t_ref[...]
    rows[...] = jnp.zeros_like(rows)
    columns = jnp.zeros((SPAN, SPAN), f32)
    d_scores = jnp.zeros((SPAN, SPAN), f32)
    for pair in range(PAIRS):
        cut = slice(pair * SPAN, (pair + 1) * SPAN)
        values = active[:, cut]
        d_mixed = dmixed_ref[:, cut]
        d_low = d_mixed.astype(low)
        d_weights = nt(d_low, diagonal(values, mask))
        weights = []
        for half in range(2):
            h = 2 * pair + half
            decay = decay_of(cumul, cumul_t, h, causal)
            step_row = step_t[h : h + 1, :]
            part = d_weights[:, half * SPAN : (half + 1) * SPAN] * decay
            d_scores = d_scores + part * step_row
            scored = part * scores
            rows[h : h + 1, :] = jnp.sum(scored, axis=0, keepdims=True)
            along = jnp.sum(scored * step_row, axis=1, keepdims=True)
            columns = jnp.where(lane == h, along, columns)
            weights.append((scores * decay * step_row).astype(low))
        back = tn(jnp.concatenate(weights, axis=1), d_low)
        dvalues_ref[:, cut] = (
            jnp.where(mask, back[:SPAN], back[SPAN:]) + skip_ref[:, cut] * d_mixed
        )
    d_step = rows[...].T
    dstep_ref[...] = d_step
    dcumul_ref[...] = columns - d_step * step_ref[...]
    d_low = d_scores.astype(low)
    dbc_ref[:, :NSTATE] = tn(d_low, readout)
    dbc_ref[:, NSTATE:] = nn(d_low, inputs_b)


def finish_kernel(
    pre_ref, cumul_ref, step_ref, sigma_ref, dmixed_ref, start_ref, after_ref,
    dvalues_ref, dstep_ref, dcumul_ref, dinter_ref, dbc_ref, cs_ref, halo_ref, taps_ref,
    head_ref, fold_ref,
    dconv_ref, dpre_ref, edge_ref, sums_ref, heads_ref,
    padded, shifted, lead,
):
    first = pl.program_id(1) == 0

    @pl.when(first & (pl.program_id(0) == 0))
    def _():
        sums_ref[...] = jnp.zeros_like(sums_ref)
        heads_ref[...] = jnp.zeros_like(heads_ref)

    pre = pre_ref[...]
    sigma = jax.nn.sigmoid(pre)
    active = pre * sigma
    values = active[:, :INNER]
    inputs_b = active[:, INNER : INNER + NSTATE].astype(low)
    cumul, step = cumul_ref[...], step_ref[...]
    after = after_ref[0]
    start = start_ref[0]
    after_low = after.astype(low)
    last = cumul[SPAN - 1 : SPAN, :]
    expo_tail = jnp.exp(last - cumul)
    tail = expo_tail * step
    tail_wide = expand(tail)
    fold = fold_ref[...]
    q = nn(inputs_b, after_low)
    d_values = dvalues_ref[...] + tail_wide * q
    d_b = dbc_ref[:, :NSTATE] + nt((tail_wide * values).astype(low), after_low)
    grown = (expand(jnp.exp(cumul)) * dmixed_ref[...]).astype(low)
    d_c = dbc_ref[:, NSTATE:] + nt(grown, start.astype(low))
    d_tail = head_sum(values * q, fold)
    tail_term = d_tail * tail
    d_step = dstep_ref[...] + d_tail * expo_tail
    d_cumul = dcumul_ref[...] + dinter_ref[...] - tail_term
    both = jnp.broadcast_to(jnp.sum(after * start, axis=0, keepdims=True), (8, INNER))
    end = jnp.exp(last) * head_sum(both, fold)[0:1, :] + jnp.sum(
        tail_term, axis=0, keepdims=True
    )
    row = lax.broadcasted_iota(jnp.int32, (SPAN, SPAN), 0)
    column = lax.broadcasted_iota(jnp.int32, (SPAN, SPAN), 1)
    upper = (row <= column).astype(f32)
    d_log = nn(upper, d_cumul, lax.Precision.HIGHEST) + end
    rate = -jnp.exp(head_ref[1:2, :])
    d_pre = (d_step + d_log * rate) * sigma_ref[...]
    d_pre = jnp.where(column < HEADS, d_pre, 0.0)
    dpre_ref[...] = d_pre
    heads_ref[0:1, :] += jnp.sum(d_log * step, axis=0, keepdims=True) * rate
    heads_ref[1:2, :] += jnp.sum(d_pre, axis=0, keepdims=True)
    d_active = jnp.concatenate([d_values, d_b, d_c], axis=1)
    d_conv = d_active * (sigma * (1.0 + pre * (1.0 - sigma)))

    @pl.when(first)
    def _():
        shifted[SPAN:, :] = jnp.zeros((8, XBC), f32)

    @pl.when(jnp.logical_not(first))
    def _():
        shifted[SPAN:, :] = shifted[0:8, :]

    shifted[0:SPAN, :] = d_conv
    padded[0:8, :] = halo_ref[0]
    padded[8:, :] = cs_ref[:, :XBC].astype(f32)
    lead[0:8, :] = jnp.zeros((8, XBC), f32)
    lead[8:, :] = d_conv[0:8, :]
    dconv_ref[...] = sum(
        taps_ref[k : k + 1, :] * shifted[3 - k : 3 - k + SPAN, :] for k in range(CONV)
    )
    edge_ref[0] = sum(taps_ref[k : k + 1, :] * lead[8 - k : 16 - k, :] for k in range(CONV))
    for k in range(CONV):
        sums_ref[k : k + 1, :] += jnp.sum(
            d_conv * padded[5 + k : 5 + k + SPAN, :], axis=0, keepdims=True
        )
    sums_ref[CONV : CONV + 1, :] += jnp.sum(d_conv, axis=0, keepdims=True)


def call(kernel, grid, operands, results, scratch=(), backwards=False, flops=0):
    seqs, spans = grid

    def spec(kind, shape):
        if kind == "all":
            return pl.BlockSpec(shape, lambda b, c: (0,) * len(shape))
        if kind == "seq":
            return pl.BlockSpec((1,) + shape[1:], lambda b, c: (b, 0, 0))

        def at(b, c):
            return b * spans + ((spans - 1 - c) if backwards else c)

        if kind == "span":
            return pl.BlockSpec((1,) + shape[1:], lambda b, c: (at(b, c), 0, 0))
        return pl.BlockSpec((SPAN,) + shape[1:], lambda b, c: (at(b, c), 0))

    arrays = [array for _, array in operands]
    moved = sum(a.size * a.dtype.itemsize for a in arrays)
    return pl.pallas_call(
        kernel,
        grid=grid,
        in_specs=[spec(kind, array.shape) for kind, array in operands],
        out_specs=[spec(kind, shape) for kind, shape, _ in results],
        out_shape=[jax.ShapeDtypeStruct(shape, kept) for _, shape, kept in results],
        scratch_shapes=[pltpu.VMEM(shape, f32) for shape in scratch],
        compiler_params=pltpu.CompilerParams(vmem_limit_bytes=50 * 1024 * 1024),
        cost_estimate=pl.CostEstimate(
            flops=flops, bytes_accessed=2 * moved, transcendentals=0
        ),
    )(*arrays)


def passed_along(block, axis, distance):
    devices = range(lax.axis_size(axis))
    route = [(i - distance, i) for i in devices if i - distance in devices]
    return lax.ppermute(block, axis, route)


def carried_in(decay, state, reverse):
    count = lax.axis_size("ctx")
    place = lax.axis_index("ctx")
    high = lax.reduce_precision(decay, 8, 7)
    extra = jnp.stack([high, decay - high], axis=1)
    sent = jnp.concatenate([state, extra], axis=1).astype(low)
    sent = jnp.pad(sent, ((0, 0), (0, TAIL_ROWS - 2), (0, 0)))
    gathered = lax.all_gather(sent, "ctx")
    entering = jnp.zeros(state.shape, f32)
    for lap in range(count - 1):
        source = count - 1 - lap if reverse else lap
        member = gathered[source].astype(f32)
        scale = member[:, NSTATE : NSTATE + 1] + member[:, NSTATE + 1 : NSTATE + 2]
        passed = scale * entering + member[:, :NSTATE]
        wanted = source > place if reverse else source < place
        entering = jnp.where(wanted, passed, entering)
    return entering


def packed(parts, rows):
    flat = jnp.concatenate([part.reshape(part.shape[0], -1) for part in parts], axis=1)
    return jnp.pad(flat, ((0, 0), (0, rows * SPARE - flat.shape[1]))).reshape(-1, SPARE)


def gather_weights(norm_weight, in_weight, conv_weight, conv_bias, gated_gain, out_weight):
    rows = in_weight.shape[0]
    owners = lax.axis_size("dp")
    members = (norm_weight, conv_weight, conv_bias, gated_gain)
    small = packed([part.reshape(1, -1) for part in members], rows)
    conv_part = lax.all_gather(
        jnp.concatenate([in_weight[:, INNER:], small], axis=1), "dp", axis=0, tiled=True
    )
    gate_part = lax.all_gather(in_weight[:, :INNER], "dp", axis=0, tiled=True)
    out_full = lax.all_gather(out_weight, "dp", axis=0, tiled=True)
    spare = conv_part[:, WIDE - SPARE :].reshape(owners, rows * SPARE)
    cut = 0
    fields = []
    for member in members:
        fields.append(spare[:, cut : cut + member.size])
        cut += member.size
    conv_full = jnp.swapaxes(fields[1].reshape(owners, CONV, -1), 0, 1).reshape(CONV, -1)
    return (
        fields[0].reshape(1, -1).astype(f32),
        conv_part,
        gate_part,
        conv_full.astype(f32),
        fields[2].reshape(1, -1).astype(f32),
        fields[3].reshape(1, -1).astype(f32),
        out_full,
    )


def scattered(grad):
    part = lax.psum_scatter(grad.astype(low), "dp", scatter_dimension=0, tiled=True)
    return lax.psum(part, "ctx").astype(f32)


def on_device(
    tokens,
    norm_weight,
    in_weight,
    conv_weight,
    conv_bias,
    decay_log,
    skip_gain,
    step_bias,
    gated_gain,
    out_weight,
    cotangent,
):
    seqs, length, width = tokens.shape
    count = seqs * length
    spans = length // SPAN
    grid = (seqs, spans)
    blocks = seqs * spans
    owners = lax.axis_size("dp")
    norm_row, conv_part, gate_part, taps, bias, gain, out_full = gather_weights(
        norm_weight, in_weight, conv_weight, conv_bias, gated_gain, out_weight
    )
    stream = tokens.reshape(count, width).astype(f32)
    cotan = cotangent.reshape(count, width)
    inv_rms = lax.rsqrt(jnp.mean(stream * stream, axis=-1, keepdims=True) + epsilon)
    normed = (stream * inv_rms * norm_row).astype(low)
    cs = nn(normed, conv_part).astype(low)
    conv_in = cs[:, :XBC].reshape(seqs, spans, SPAN, XBC)
    ends = conv_in[:, :, SPAN - CONV + 1 :]
    edge = passed_along(ends[:, -1], "ctx", 1)
    halo = jnp.concatenate([edge[:, None], ends[:, :-1]], axis=1).astype(f32)
    halo = jnp.pad(halo, ((0, 0), (0, 0), (8 - CONV + 1, 0), (0, 0))).reshape(blocks, 8, XBC)
    head_rows = jnp.pad(jnp.stack([step_bias, decay_log]), ((0, 6), (0, SPAN - HEADS)))
    skip_row = jnp.repeat(skip_gain, HEADDIM)[None]
    fold = (jnp.arange(INNER)[:, None] // HEADDIM == jnp.arange(SPAN)[None]).astype(low)
    square = ("row", (count, SPAN), f32)
    state_shape = ("span", (blocks, NSTATE, INNER), f32)
    pre, cumul, cumul_t, step, step_t, sigma, update, decay = call(
        prepare_kernel,
        grid,
        [("row", cs), ("span", halo), ("all", taps), ("all", bias), ("all", head_rows)],
        [("row", (count, XBC), f32)] + [square] * 5 + [state_shape, ("span", (blocks, 8, INNER), f32)],
        [(SPAN + 8, XBC)],
        flops=blocks * 60_000_000,
    )
    decay = decay[:, :1].reshape(seqs, spans, 1, INNER)
    update = update.reshape(seqs, spans, NSTATE, INNER)
    total, total_decay = update[:, 0], decay[:, 0]
    for c in range(1, spans):
        total = decay[:, c] * total + update[:, c]
        total_decay = total_decay * decay[:, c]
    entering = carried_in(total_decay[:, 0], total, False)
    partial, = call(
        intra_kernel,
        grid,
        [("row", pre), ("row", cumul), ("row", cumul_t), ("row", step_t), ("all", skip_row)],
        [("row", (count, INNER), f32)],
        flops=blocks * 300_000_000,
    )
    gate_raw = nn(normed, gate_part).astype(low)
    d_gated = nt(cotan, out_full)
    starts = [entering]
    for c in range(spans - 1):
        starts.append(decay[:, c] * starts[-1] + update[:, c])
    starts = jnp.stack(starts, axis=1).reshape(blocks, NSTATE, INNER)
    gated, d_gate_raw, d_mixed, d_start, d_inter, gate_sums = call(
        gate_kernel,
        grid,
        [
            ("row", partial), ("row", pre), ("row", cumul), ("span", starts), ("row", gate_raw),
            ("row", d_gated), ("all", gain), ("all", fold),
        ],
        [
            ("row", (count, INNER), low), ("row", (count, INNER), low),
            ("row", (count, INNER), f32), state_shape, square, ("all", (8, INNER), f32),
        ],
        flops=blocks * 200_000_000,
    )
    d_start = d_start.reshape(seqs, spans, NSTATE, INNER)
    lead = d_start[:, spans - 1]
    for c in range(spans - 2, -1, -1):
        lead = d_start[:, c] + decay[:, c] * lead
    arriving = carried_in(total_decay[:, 0], lead, True)
    out_grad = tn(gated, cotan)
    block_output = (stream + nn(gated, out_full)).astype(low)
    out_part = scattered(out_grad)
    gate_grad = scattered(tn(normed, d_gate_raw))
    d_values, d_step, d_cumul, d_bc = call(
        local_kernel,
        grid,
        [
            ("row", pre), ("row", cumul), ("row", cumul_t), ("row", step), ("row", step_t),
            ("row", d_mixed), ("all", skip_row),
        ],
        [("row", (count, INNER), f32), square, square, ("row", (count, 2 * NSTATE), f32)],
        [(SPAN, SPAN)],
        flops=blocks * 500_000_000,
    )
    after = [arriving]
    for c in range(spans - 1, 0, -1):
        after.append(d_start[:, c] + decay[:, c] * after[-1])
    after = jnp.stack(after[::-1], axis=1).reshape(blocks, NSTATE, INNER)
    d_conv_in, d_step_pre, back_rows, conv_sums, head_sums = call(
        finish_kernel,
        grid,
        [
            ("row", pre), ("row", cumul), ("row", step), ("row", sigma), ("row", d_mixed),
            ("span", starts), ("span", after), ("row", d_values), ("row", d_step),
            ("row", d_cumul), ("row", d_inter), ("row", d_bc), ("row", cs), ("span", halo),
            ("all", taps), ("all", head_rows), ("all", fold),
        ],
        [
            ("row", (count, XBC), f32), square, ("seq", (seqs, 8, XBC), f32),
            ("all", (8, XBC), f32), ("all", (8, SPAN), f32),
        ],
        [(SPAN + 8, XBC), (SPAN + 8, XBC), (16, XBC)],
        backwards=True,
        flops=blocks * 200_000_000,
    )
    heads = jnp.concatenate(
        [
            head_sums[0, :HEADS],
            jnp.sum(gate_sums[1].reshape(HEADS, HEADDIM), axis=1),
            head_sums[1, :HEADS],
        ]
    )
    heads = lax.psum(heads, ("dp", "ctx")).reshape(3, HEADS)
    back_edge = passed_along(back_rows[:, : CONV - 1], "ctx", -1)
    d_conv_in = d_conv_in.reshape(seqs, length, XBC) + jnp.pad(
        back_edge, ((0, 0), (length - CONV + 1, 0), (0, 0))
    )
    d_cs = jnp.concatenate([d_conv_in.reshape(count, XBC), d_step_pre], axis=1).astype(low)
    d_normed = nt(d_cs, conv_part) + nt(d_gate_raw, gate_part)
    norm_grad = jnp.sum(d_normed * stream * inv_rms, axis=0)
    d_hat = d_normed * norm_row
    d_stream = inv_rms * d_hat - stream * inv_rms**3 * jnp.mean(
        d_hat * stream, axis=-1, keepdims=True
    )
    input_grad = (cotan.astype(f32) + d_stream).astype(low)
    members = (
        norm_grad.reshape(owners, -1),
        jnp.swapaxes(conv_sums[:CONV].reshape(CONV, owners, -1), 0, 1).reshape(owners, -1),
        conv_sums[CONV].reshape(owners, -1),
        gate_sums[0].reshape(owners, -1),
    )
    small = packed(members, width // owners)
    conv_grad = scattered(jnp.concatenate([tn(normed, d_cs)[:, : WIDE - SPARE], small], axis=1))
    spare = conv_grad[:, WIDE - SPARE :].reshape(-1)
    cut = 0
    fields = []
    for member in members:
        fields.append(spare[cut : cut + member.shape[1]])
        cut += member.shape[1]
    return (
        block_output.reshape(seqs, length, width),
        input_grad.reshape(seqs, length, width),
        fields[0],
        jnp.concatenate([gate_grad, conv_grad[:, : WIDE - SPARE]], axis=1),
        fields[1].reshape(CONV, -1),
        fields[2],
        heads[0],
        heads[1],
        heads[2],
        fields[3],
        out_part,
    )


def solution(mesh):
    return jax.shard_map(
        on_device,
        mesh=mesh,
        in_specs=(
            P("dp", "ctx", None),
            P("dp"),
            P("dp", None),
            P(None, "dp"),
            P("dp"),
            P(),
            P(),
            P(),
            P("dp"),
            P("dp", None),
            P("dp", "ctx", None),
        ),
        out_specs=(
            P("dp", "ctx", None),
            P("dp", "ctx", None),
            P("dp"),
            P("dp", None),
            P(None, "dp"),
            P("dp"),
            P(),
            P(),
            P(),
            P("dp"),
            P("dp", None),
        ),
        check_vma=False,
    )
```

```python
import jax
import jax.numpy as jnp
from jax import lax
from jax.experimental import pallas as pl
from jax.experimental.pallas import tpu as pltpu
from jax.sharding import PartitionSpec as P

HEADS = 24
HEADDIM = 64
NSTATE = 128
CONV = 4
SPAN = 128
INNER = 1536
XBC = 1792
WIDE = 1920
SPARE = 104
PAIRS = HEADS // 2
TAIL_ROWS = 16

epsilon = 1e-05
low = jnp.bfloat16
f32 = jnp.float32


def nn(a, b, precision=None):
    return lax.dot_general(
        a, b, (((1,), (0,)), ((), ())), precision=precision, preferred_element_type=f32
    )


def nt(a, b):
    return lax.dot_general(a, b, (((1,), (1,)), ((), ())), preferred_element_type=f32)


def tn(a, b):
    return lax.dot_general(a, b, (((0,), (0,)), ((), ())), preferred_element_type=f32)


def silu_grad(pre):
    sigma = jax.nn.sigmoid(pre)
    return sigma * (1.0 + pre * (1.0 - sigma))


def first_half(rows):
    return lax.broadcasted_iota(jnp.int32, (rows, SPAN), 1) < HEADDIM


def expand(per_head):
    rows = per_head.shape[0]
    mask = first_half(rows)
    pieces = []
    for pair in range(PAIRS):
        left = jnp.broadcast_to(per_head[:, 2 * pair : 2 * pair + 1], (rows, SPAN))
        right = jnp.broadcast_to(per_head[:, 2 * pair + 1 : 2 * pair + 2], (rows, SPAN))
        pieces.append(jnp.where(mask, left, right))
    return jnp.concatenate(pieces, axis=1)


def head_sum(wide, fold):
    high = wide.astype(low)
    rest = (wide - high.astype(f32)).astype(low)
    return nn(high, fold) + nn(rest, fold)


def diagonal(block, mask):
    zero = jnp.zeros_like(block)
    return jnp.concatenate(
        [jnp.where(mask, block, zero), jnp.where(mask, zero, block)], axis=0
    ).astype(low)


def causal_mask():
    row = lax.broadcasted_iota(jnp.int32, (SPAN, SPAN), 0)
    column = lax.broadcasted_iota(jnp.int32, (SPAN, SPAN), 1)
    return row >= column


def decay_of(cumul, cumul_t, head, causal):
    gap = cumul[:, head : head + 1] - cumul_t[head : head + 1, :]
    return jnp.exp(jnp.where(causal, gap, -1e30))


def prepare_kernel(
    cs_ref, halo_ref, taps_ref, bias_ref, head_ref,
    pre_ref, cumul_ref, cumul_t_ref, step_ref, step_t_ref, sigma_ref, update_ref, decay_ref,
    padded,
):
    padded[0:8, :] = halo_ref[0]
    padded[8:, :] = cs_ref[:, :XBC].astype(f32)
    pre = bias_ref[...] + sum(
        padded[5 + k : 5 + k + SPAN, :] * taps_ref[k : k + 1, :] for k in range(CONV)
    )
    pre_ref[...] = pre
    active = pre * jax.nn.sigmoid(pre)
    values = active[:, :INNER]
    inputs_b = active[:, INNER : INNER + NSTATE].astype(low)
    lane = lax.broadcasted_iota(jnp.int32, (SPAN, SPAN), 1)
    raw = jnp.where(lane < HEADS, cs_ref[:, XBC:].astype(f32) + head_ref[0:1, :], 0.0)
    step = jnp.maximum(raw, 0.0) + jnp.log1p(jnp.exp(-jnp.abs(raw)))
    step = jnp.where(lane < HEADS, step, 0.0)
    sigma_ref[...] = jax.nn.sigmoid(raw)
    log_step = step * (-jnp.exp(head_ref[1:2, :]))
    lower = causal_mask().astype(f32)
    cumul = nn(lower, log_step, lax.Precision.HIGHEST)
    cumul_ref[...] = cumul
    step_ref[...] = step
    cumul_t_ref[...] = cumul.T
    step_t_ref[...] = step.T
    last = cumul[SPAN - 1 : SPAN, :]
    tail = jnp.exp(last - cumul) * step
    update_ref[0] = tn(inputs_b, (expand(tail) * values).astype(low))
    decay_ref[0] = jnp.broadcast_to(expand(jnp.exp(last)), (8, INNER))


def intra_kernel(pre_ref, cumul_ref, cumul_t_ref, step_t_ref, skip_ref, out_ref):
    pre = pre_ref[...]
    active = pre * jax.nn.sigmoid(pre)
    inputs_b = active[:, INNER : INNER + NSTATE].astype(low)
    readout = active[:, INNER + NSTATE :].astype(low)
    scores = nt(readout, inputs_b)
    causal = causal_mask()
    mask = first_half(SPAN)
    cumul, cumul_t, step_t = cumul_ref[...], cumul_t_ref[...], step_t_ref[...]
    for pair in range(PAIRS):
        cut = slice(pair * SPAN, (pair + 1) * SPAN)
        values = active[:, cut]
        weights = [
            (scores * decay_of(cumul, cumul_t, h, causal) * step_t[h : h + 1, :]).astype(low)
            for h in (2 * pair, 2 * pair + 1)
        ]
        inner = nn(jnp.concatenate(weights, axis=1), diagonal(values, mask))
        out_ref[:, cut] = inner + skip_ref[:, cut] * values


def gate_kernel(
    partial_ref, pre_ref, cumul_ref, start_ref, gate_ref, dgated_ref, gain_ref, fold_ref,
    gated_ref, dgate_ref, dmixed_ref, dstart_ref, dcumul_ref, sums_ref,
):
    @pl.when((pl.program_id(0) == 0) & (pl.program_id(1) == 0))
    def _():
        sums_ref[...] = jnp.zeros_like(sums_ref)

    pre = pre_ref[...]
    active = pre * jax.nn.sigmoid(pre)
    values = active[:, :INNER]
    readout = active[:, INNER + NSTATE :].astype(low)
    growth = expand(jnp.exp(cumul_ref[...]))
    inter = growth * nn(readout, start_ref[0].astype(low))
    mixed = partial_ref[...] + inter
    gate = gate_ref[...].astype(f32)
    sigma = jax.nn.sigmoid(gate)
    act = gate * sigma
    gate_val = mixed * act
    rms = lax.rsqrt(jnp.mean(gate_val * gate_val, axis=1, keepdims=True) + epsilon)
    hat = gate_val * rms
    gain = gain_ref[...]
    gated_ref[...] = (hat * gain).astype(low)
    d_gated = dgated_ref[...]
    sums_ref[0:1, :] += jnp.sum(d_gated * hat, axis=0, keepdims=True)
    d_hat = d_gated * gain
    d_gate = rms * d_hat - hat * (rms * rms * jnp.mean(d_hat * gate_val, axis=1, keepdims=True))
    dgate_ref[...] = (d_gate * mixed * (sigma * (1.0 + gate * (1.0 - sigma)))).astype(low)
    d_mixed = d_gate * act
    dmixed_ref[...] = d_mixed
    sums_ref[1:2, :] += jnp.sum(d_mixed * values, axis=0, keepdims=True)
    dstart_ref[0] = tn(readout, (growth * d_mixed).astype(low))
    dcumul_ref[...] = head_sum(d_mixed * inter, fold_ref[...])


def local_kernel(
    pre_ref, cumul_ref, cumul_t_ref, step_ref, step_t_ref, dmixed_ref, skip_ref,
    dvalues_ref, dstep_ref, dcumul_ref, dbc_ref, rows,
):
    pre = pre_ref[...]
    active = pre * jax.nn.sigmoid(pre)
    inputs_b = active[:, INNER : INNER + NSTATE].astype(low)
    readout = active[:, INNER + NSTATE :].astype(low)
    scores = nt(readout, inputs_b)
    causal = causal_mask()
    mask = first_half(SPAN)
    lane = lax.broadcasted_iota(jnp.int32, (SPAN, SPAN), 1)
    cumul, cumul_t, step_t = cumul_ref[...], cumul_t_ref[...], step_t_ref[...]
    rows[...] = jnp.zeros_like(rows)
    columns = jnp.zeros((SPAN, SPAN), f32)
    d_scores = jnp.zeros((SPAN, SPAN), f32)
    for pair in range(PAIRS):
        cut = slice(pair * SPAN, (pair + 1) * SPAN)
        values = active[:, cut]
        d_mixed = dmixed_ref[:, cut]
        d_low = d_mixed.astype(low)
        d_weights = nt(d_low, diagonal(values, mask))
        weights = []
        for half in range(2):
            h = 2 * pair + half
            decay = decay_of(cumul, cumul_t, h, causal)
            step_row = step_t[h : h + 1, :]
            part = d_weights[:, half * SPAN : (half + 1) * SPAN] * decay
            d_scores = d_scores + part * step_row
            scored = part * scores
            rows[h : h + 1, :] = jnp.sum(scored, axis=0, keepdims=True)
            along = jnp.sum(scored * step_row, axis=1, keepdims=True)
            columns = jnp.where(lane == h, along, columns)
            weights.append((scores * decay * step_row).astype(low))
        back = tn(jnp.concatenate(weights, axis=1), d_low)
        dvalues_ref[:, cut] = (
            jnp.where(mask, back[:SPAN], back[SPAN:]) + skip_ref[:, cut] * d_mixed
        )
    d_step = rows[...].T
    dstep_ref[...] = d_step
    dcumul_ref[...] = columns - d_step * step_ref[...]
    d_low = d_scores.astype(low)
    dbc_ref[:, :NSTATE] = tn(d_low, readout)
    dbc_ref[:, NSTATE:] = nn(d_low, inputs_b)


def finish_kernel(
    pre_ref, cumul_ref, step_ref, sigma_ref, dmixed_ref, start_ref, after_ref,
    dvalues_ref, dstep_ref, dcumul_ref, dinter_ref, dbc_ref, cs_ref, halo_ref, taps_ref,
    head_ref, fold_ref,
    dconv_ref, dpre_ref, edge_ref, sums_ref, heads_ref,
    padded, shifted, lead,
):
    first = pl.program_id(1) == 0

    @pl.when(first & (pl.program_id(0) == 0))
    def _():
        sums_ref[...] = jnp.zeros_like(sums_ref)
        heads_ref[...] = jnp.zeros_like(heads_ref)

    pre = pre_ref[...]
    sigma = jax.nn.sigmoid(pre)
    active = pre * sigma
    values = active[:, :INNER]
    inputs_b = active[:, INNER : INNER + NSTATE].astype(low)
    cumul, step = cumul_ref[...], step_ref[...]
    after = after_ref[0]
    start = start_ref[0]
    after_low = after.astype(low)
    last = cumul[SPAN - 1 : SPAN, :]
    expo_tail = jnp.exp(last - cumul)
    tail = expo_tail * step
    tail_wide = expand(tail)
    fold = fold_ref[...]
    q = nn(inputs_b, after_low)
    d_values = dvalues_ref[...] + tail_wide * q
    d_b = dbc_ref[:, :NSTATE] + nt((tail_wide * values).astype(low), after_low)
    grown = (expand(jnp.exp(cumul)) * dmixed_ref[...]).astype(low)
    d_c = dbc_ref[:, NSTATE:] + nt(grown, start.astype(low))
    d_tail = head_sum(values * q, fold)
    tail_term = d_tail * tail
    d_step = dstep_ref[...] + d_tail * expo_tail
    d_cumul = dcumul_ref[...] + dinter_ref[...] - tail_term
    both = jnp.broadcast_to(jnp.sum(after * start, axis=0, keepdims=True), (8, INNER))
    end = jnp.exp(last) * head_sum(both, fold)[0:1, :] + jnp.sum(
        tail_term, axis=0, keepdims=True
    )
    row = lax.broadcasted_iota(jnp.int32, (SPAN, SPAN), 0)
    column = lax.broadcasted_iota(jnp.int32, (SPAN, SPAN), 1)
    upper = (row <= column).astype(f32)
    d_log = nn(upper, d_cumul, lax.Precision.HIGHEST) + end
    rate = -jnp.exp(head_ref[1:2, :])
    d_pre = (d_step + d_log * rate) * sigma_ref[...]
    d_pre = jnp.where(column < HEADS, d_pre, 0.0)
    dpre_ref[...] = d_pre
    heads_ref[0:1, :] += jnp.sum(d_log * step, axis=0, keepdims=True) * rate
    heads_ref[1:2, :] += jnp.sum(d_pre, axis=0, keepdims=True)
    d_active = jnp.concatenate([d_values, d_b, d_c], axis=1)
    d_conv = d_active * (sigma * (1.0 + pre * (1.0 - sigma)))

    @pl.when(first)
    def _():
        shifted[SPAN:, :] = jnp.zeros((8, XBC), f32)

    @pl.when(jnp.logical_not(first))
    def _():
        shifted[SPAN:, :] = shifted[0:8, :]

    shifted[0:SPAN, :] = d_conv
    padded[0:8, :] = halo_ref[0]
    padded[8:, :] = cs_ref[:, :XBC].astype(f32)
    lead[0:8, :] = jnp.zeros((8, XBC), f32)
    lead[8:, :] = d_conv[0:8, :]
    dconv_ref[...] = sum(
        taps_ref[k : k + 1, :] * shifted[3 - k : 3 - k + SPAN, :] for k in range(CONV)
    )
    edge_ref[0] = sum(taps_ref[k : k + 1, :] * lead[8 - k : 16 - k, :] for k in range(CONV))
    for k in range(CONV):
        sums_ref[k : k + 1, :] += jnp.sum(
            d_conv * padded[5 + k : 5 + k + SPAN, :], axis=0, keepdims=True
        )
    sums_ref[CONV : CONV + 1, :] += jnp.sum(d_conv, axis=0, keepdims=True)


def call(kernel, grid, operands, results, scratch=(), backwards=False, flops=0):
    seqs, spans = grid

    def spec(kind, shape):
        if kind == "all":
            return pl.BlockSpec(shape, lambda b, c: (0,) * len(shape))
        if kind == "seq":
            return pl.BlockSpec((1,) + shape[1:], lambda b, c: (b, 0, 0))

        def at(b, c):
            return b * spans + ((spans - 1 - c) if backwards else c)

        if kind == "span":
            return pl.BlockSpec((1,) + shape[1:], lambda b, c: (at(b, c), 0, 0))
        return pl.BlockSpec((SPAN,) + shape[1:], lambda b, c: (at(b, c), 0))

    arrays = [array for _, array in operands]
    moved = sum(a.size * a.dtype.itemsize for a in arrays)
    return pl.pallas_call(
        kernel,
        grid=grid,
        in_specs=[spec(kind, array.shape) for kind, array in operands],
        out_specs=[spec(kind, shape) for kind, shape, _ in results],
        out_shape=[jax.ShapeDtypeStruct(shape, kept) for _, shape, kept in results],
        scratch_shapes=[pltpu.VMEM(shape, f32) for shape in scratch],
        compiler_params=pltpu.CompilerParams(vmem_limit_bytes=50 * 1024 * 1024),
        cost_estimate=pl.CostEstimate(
            flops=flops, bytes_accessed=2 * moved, transcendentals=0
        ),
    )(*arrays)


def passed_along(block, axis, distance):
    devices = range(lax.axis_size(axis))
    route = [(i - distance, i) for i in devices if i - distance in devices]
    return lax.ppermute(block, axis, route)


def carried_in(decay, state, reverse):
    count = lax.axis_size("ctx")
    place = lax.axis_index("ctx")
    high = lax.reduce_precision(decay, 8, 7)
    extra = jnp.stack([high, decay - high], axis=1)
    sent = jnp.concatenate([state, extra], axis=1).astype(low)
    sent = jnp.pad(sent, ((0, 0), (0, TAIL_ROWS - 2), (0, 0)))
    gathered = lax.all_gather(sent, "ctx")
    entering = jnp.zeros(state.shape, f32)
    for lap in range(count - 1):
        source = count - 1 - lap if reverse else lap
        member = gathered[source].astype(f32)
        scale = member[:, NSTATE : NSTATE + 1] + member[:, NSTATE + 1 : NSTATE + 2]
        passed = scale * entering + member[:, :NSTATE]
        wanted = source > place if reverse else source < place
        entering = jnp.where(wanted, passed, entering)
    return entering


COLUMNS = 5120
MESH = pl.DeviceIdType.MESH


def power(size):
    return size.bit_length() - 1


def orders():
    ctx = [("ctx", bit) for bit in range(power(lax.axis_size("ctx")))]
    own = [("dp", bit) for bit in range(power(lax.axis_size("dp")))]
    return (
        ctx + own[1:2] + own[:1] + own[2:],
        ctx[:1] + own[:1] + ctx[1:] + own[1:],
    )


def bit_of(axis, bit):
    return lax.axis_index(axis) // 2**bit % 2


def partner(axis, bit):
    dp, ctx = lax.axis_index("dp"), lax.axis_index("ctx")
    move = 2**bit * (1 - 2 * bit_of(axis, bit))
    return (dp + move, ctx) if axis == "dp" else (dp, ctx + move)


def greet(steps):
    barrier = pltpu.get_barrier_semaphore()
    for axis, bit in steps:
        pl.semaphore_signal(
            barrier, inc=1, device_id=partner(axis, bit), device_id_type=MESH
        )
    pl.semaphore_wait(barrier, len(steps))


def own_index(steps):
    index = 0
    for axis, bit in steps:
        index = index * 2 + bit_of(axis, bit)
    return index


def remote(source, target, sends, receives, slot, axis, bit):
    return pltpu.make_async_remote_copy(
        src_ref=source,
        dst_ref=target,
        send_sem=sends.at[slot],
        recv_sem=receives.at[slot],
        device_id=partner(axis, bit),
        device_id_type=MESH,
    )


def spread_kernel(plans, first_ref, second_ref, first_out, second_out, local, sends, receives):
    count = len(plans[0])
    outs = (first_out, second_out)
    offsets = [own_index(plan) for plan in plans]
    places = []
    for stream, source in enumerate((first_ref, second_ref)):
        place = pltpu.make_async_copy(
            source, outs[stream].at[pl.ds(offsets[stream], 1)], local.at[stream]
        )
        place.start()
        places.append(place)
    greet(plans[0])
    copies = [[], []]

    def launch(stream, step):
        axis, bit = plans[stream][count - 1 - step]
        region = outs[stream].at[pl.ds(offsets[stream], 2**step)]
        copy = remote(region, region, sends, receives, stream * count + step, axis, bit)
        copy.start()
        copies[stream].append(copy)

    for stream in range(2):
        places[stream].wait()
        launch(stream, 0)
    for step in range(count):
        for stream in range(2):
            axis, bit = plans[stream][count - 1 - step]
            copies[stream][step].wait_recv()
            offsets[stream] = offsets[stream] - bit_of(axis, bit) * 2**step
            if step < count - 1:
                launch(stream, step + 1)
    for stream in range(2):
        for copy in copies[stream]:
            copy.wait_send()


def merge_kernel(
    plans, deep, first_ref, second_ref, heads_ref, first_out, second_out, heads_out,
    sums, arrived, final, head_sums, head_arrived,
    sends, receives, last_sends, last_receives, head_sends, head_receives,
):
    count = len(plans[0])
    pieces = 2**count
    refs = (first_ref, second_ref)
    outs = (first_out, second_out)
    greet(plans[0])
    offsets = [0, 0]
    copies = [[], []]
    head_copies = []
    head_sums[0] = heads_ref[...]

    def launch(stream, step):
        axis, bit = plans[stream][step]
        half = pieces // 2 ** (step + 1)
        away = offsets[stream] + (1 - bit_of(axis, bit)) * half
        held = refs[stream] if step == 0 else sums.at[stream]
        copy = remote(
            held.at[pl.ds(away, half)],
            arrived.at[stream, pl.ds(pieces - 2 * half, half)],
            sends, receives, stream * count + step, axis, bit,
        )
        copy.start()
        copies[stream].append(copy)

    def launch_heads(step):
        axis, bit = plans[0][step]
        copy = remote(
            head_sums.at[step], head_arrived.at[step], head_sends, head_receives, step, axis, bit
        )
        copy.start()
        head_copies.append(copy)

    launch_heads(0)
    for stream in range(2):
        launch(stream, 0)
    for step in range(count):
        half = pieces // 2 ** (step + 1)
        for stream in range(2):
            axis, bit = plans[stream][step]
            copies[stream][step].wait_recv()
            keep = offsets[stream] + bit_of(axis, bit) * half
            held = refs[stream] if step == 0 else sums.at[stream]

            def add(index, carry, held=held, keep=keep, stream=stream, half=half):
                total = held[keep + index].astype(f32) + arrived[
                    stream, pieces - 2 * half + index
                ].astype(f32)
                sums[stream, keep + index] = total.astype(low)
                return carry

            lax.fori_loop(0, half, add, 0)
            offsets[stream] = keep
            if step < count - 1:
                launch(stream, step + 1)
        head_copies[step].wait_recv()
        head_sums[step + 1] = head_sums[step] + head_arrived[step]
        if step < count - 1:
            launch_heads(step + 1)
    heads_out[...] = head_sums[count]
    ctx = [("ctx", bit) for bit in range(deep)]
    at = own_index(ctx)
    last = [[], []]
    for stream in range(2):
        final[stream, at] = sums[stream, offsets[stream]]
    for step in range(deep):
        axis, bit = ctx[deep - 1 - step]
        for stream in range(2):
            region = final.at[stream, pl.ds(at, 2**step)]
            copy = remote(
                region, region, last_sends, last_receives, stream * deep + step, axis, bit
            )
            copy.start()
            last[stream].append(copy)
        for stream in range(2):
            last[stream][step].wait_recv()
        at = at - bit_of(axis, bit) * 2**step
    for stream in range(2):
        outs[stream][...] = final[stream].astype(f32)
        for copy in copies[stream] + last[stream]:
            copy.wait_send()
    for copy in head_copies:
        copy.wait_send()


def dims_of(plan):
    deep_dp = power(lax.axis_size("dp"))
    deep_ctx = power(lax.axis_size("ctx"))
    places = [
        deep_dp - 1 - bit if axis == "dp" else deep_dp + deep_ctx - bit for axis, bit in plan
    ]
    split = (2,) * deep_dp, (2,) * deep_ctx
    return split, tuple(places) + (deep_dp, deep_dp + deep_ctx + 1)


def padded_rows(rows):
    return -(-rows // 16) * 16


def spread(shard):
    rows = shard.shape[0]
    full = padded_rows(rows)
    owners, parts = lax.axis_size("dp"), lax.axis_size("ctx")
    plans = orders()
    pieces = owners * parts
    columns = COLUMNS // (2 * parts)
    shard = jnp.pad(shard, ((0, full - rows), (0, 0))).reshape(full, 2, parts, columns)
    mine = lax.dynamic_index_in_dim(shard, lax.axis_index("ctx"), 2, False)
    count = len(plans[0])
    any_spec = pl.BlockSpec(memory_space=pl.ANY)
    shape = jax.ShapeDtypeStruct((pieces, full, columns), shard.dtype)
    results = pl.pallas_call(
        lambda *refs: spread_kernel(plans, *refs),
        out_shape=[shape, shape],
        in_specs=[any_spec] * 2,
        out_specs=[any_spec] * 2,
        scratch_shapes=[
            pltpu.SemaphoreType.DMA((2,)),
            pltpu.SemaphoreType.DMA((2 * count,)),
            pltpu.SemaphoreType.DMA((2 * count,)),
        ],
        compiler_params=pltpu.CompilerParams(collective_id=0, has_side_effects=True),
    )(mine[None, :, 0], mine[None, :, 1])
    wholes = []
    for plan, result in zip(plans, results):
        split, places = dims_of(plan)
        back = sorted(range(len(places)), key=places.__getitem__)
        wide = result.reshape((2,) * count + (full, columns)).transpose(back)
        wholes.append(wide.reshape(owners, full, parts * columns))
    return jnp.concatenate(wholes, axis=2)[:, :rows]


def merged(grads, heads):
    owners, rows, _ = grads.shape
    full = padded_rows(rows)
    parts = lax.axis_size("ctx")
    plans = orders()
    pieces = owners * parts
    columns = COLUMNS // (2 * parts)
    count, deep = len(plans[0]), power(parts)
    grads = jnp.pad(grads.astype(low), ((0, 0), (0, full - rows), (0, 0)))
    streams = []
    for stream, plan in enumerate(plans):
        split, places = dims_of(plan)
        half = grads[:, :, stream * parts * columns : (stream + 1) * parts * columns]
        half = half.reshape(split[0] + (full,) + split[1] + (columns,)).transpose(places)
        streams.append(half.reshape(pieces, full, columns))
    whole = pl.BlockSpec(memory_space=pltpu.VMEM)
    shape = jax.ShapeDtypeStruct((parts, full, columns), f32)
    dma = pltpu.SemaphoreType.DMA
    first, second, heads = pl.pallas_call(
        lambda *refs: merge_kernel(plans, deep, *refs),
        out_shape=[shape, shape, jax.ShapeDtypeStruct(heads.shape, f32)],
        in_specs=[whole] * 3,
        out_specs=[whole] * 3,
        scratch_shapes=[
            pltpu.VMEM((2, pieces, full, columns), low),
            pltpu.VMEM((2, pieces, full, columns), low),
            pltpu.VMEM((2, parts, full, columns), low),
            pltpu.VMEM((count + 1,) + heads.shape, f32),
            pltpu.VMEM((count,) + heads.shape, f32),
            dma((2 * count,)),
            dma((2 * count,)),
            dma((2 * deep,)),
            dma((2 * deep,)),
            dma((count,)),
            dma((count,)),
        ],
        compiler_params=pltpu.CompilerParams(
            collective_id=1, has_side_effects=True, vmem_limit_bytes=50 * 1024 * 1024
        ),
    )(streams[0], streams[1], heads)
    wides = []
    for result in (first, second):
        wide = result.reshape((2,) * deep + (full, columns))
        wide = wide.transpose((deep,) + tuple(range(deep - 1, -1, -1)) + (deep + 1,))
        wides.append(wide.reshape(full, parts * columns))
    return jnp.concatenate(wides, axis=1)[:rows], heads


def packed(parts, rows):
    flat = jnp.concatenate([part.reshape(part.shape[0], -1) for part in parts], axis=1)
    return jnp.pad(flat, ((0, 0), (0, rows * SPARE - flat.shape[1]))).reshape(-1, SPARE)


def gather_weights(norm_weight, in_weight, conv_weight, conv_bias, gated_gain, out_weight):
    rows = in_weight.shape[0]
    owners = lax.axis_size("dp")
    members = (norm_weight, conv_weight, conv_bias, gated_gain)
    small = packed([part.reshape(1, -1) for part in members], rows)
    width = out_weight.shape[1]
    shard = jnp.concatenate(
        [in_weight[:, INNER:], small, in_weight[:, :INNER], out_weight[:rows], out_weight[rows:]],
        axis=1,
    )
    whole = spread(jnp.pad(shard, ((0, 0), (0, COLUMNS - shard.shape[1]))))
    flat = whole.reshape(owners * rows, COLUMNS)
    begin = WIDE + INNER
    out_full = jnp.stack(
        [whole[:, :, begin : begin + width], whole[:, :, begin + width : begin + 2 * width]], axis=1
    ).reshape(-1, width)
    conv_part = flat[:, :WIDE]
    spare = conv_part[:, WIDE - SPARE :].reshape(owners, rows * SPARE)
    cut = 0
    fields = []
    for member in members:
        fields.append(spare[:, cut : cut + member.size])
        cut += member.size
    conv_full = jnp.swapaxes(fields[1].reshape(owners, CONV, -1), 0, 1).reshape(CONV, -1)
    return (
        fields[0].reshape(1, -1).astype(f32),
        conv_part,
        flat[:, WIDE : WIDE + INNER],
        conv_full.astype(f32),
        fields[2].reshape(1, -1).astype(f32),
        fields[3].reshape(1, -1).astype(f32),
        out_full,
    )


def on_device(
    tokens,
    norm_weight,
    in_weight,
    conv_weight,
    conv_bias,
    decay_log,
    skip_gain,
    step_bias,
    gated_gain,
    out_weight,
    cotangent,
):
    seqs, length, width = tokens.shape
    count = seqs * length
    spans = length // SPAN
    grid = (seqs, spans)
    blocks = seqs * spans
    owners = lax.axis_size("dp")
    norm_row, conv_part, gate_part, taps, bias, gain, out_full = gather_weights(
        norm_weight, in_weight, conv_weight, conv_bias, gated_gain, out_weight
    )
    stream = tokens.reshape(count, width).astype(f32)
    cotan = cotangent.reshape(count, width)
    inv_rms = lax.rsqrt(jnp.mean(stream * stream, axis=-1, keepdims=True) + epsilon)
    normed = (stream * inv_rms * norm_row).astype(low)
    cs = nn(normed, conv_part).astype(low)
    conv_in = cs[:, :XBC].reshape(seqs, spans, SPAN, XBC)
    ends = conv_in[:, :, SPAN - CONV + 1 :]
    edge = passed_along(ends[:, -1], "ctx", 1)
    halo = jnp.concatenate([edge[:, None], ends[:, :-1]], axis=1).astype(f32)
    halo = jnp.pad(halo, ((0, 0), (0, 0), (8 - CONV + 1, 0), (0, 0))).reshape(blocks, 8, XBC)
    head_rows = jnp.pad(jnp.stack([step_bias, decay_log]), ((0, 6), (0, SPAN - HEADS)))
    skip_row = jnp.repeat(skip_gain, HEADDIM)[None]
    fold = (jnp.arange(INNER)[:, None] // HEADDIM == jnp.arange(SPAN)[None]).astype(low)
    square = ("row", (count, SPAN), f32)
    state_shape = ("span", (blocks, NSTATE, INNER), f32)
    pre, cumul, cumul_t, step, step_t, sigma, update, decay = call(
        prepare_kernel,
        grid,
        [("row", cs), ("span", halo), ("all", taps), ("all", bias), ("all", head_rows)],
        [("row", (count, XBC), f32)] + [square] * 5 + [state_shape, ("span", (blocks, 8, INNER), f32)],
        [(SPAN + 8, XBC)],
        flops=blocks * 60_000_000,
    )
    decay = decay[:, :1].reshape(seqs, spans, 1, INNER)
    update = update.reshape(seqs, spans, NSTATE, INNER)
    total, total_decay = update[:, 0], decay[:, 0]
    for c in range(1, spans):
        total = decay[:, c] * total + update[:, c]
        total_decay = total_decay * decay[:, c]
    entering = carried_in(total_decay[:, 0], total, False)
    partial, = call(
        intra_kernel,
        grid,
        [("row", pre), ("row", cumul), ("row", cumul_t), ("row", step_t), ("all", skip_row)],
        [("row", (count, INNER), f32)],
        flops=blocks * 300_000_000,
    )
    gate_raw = nn(normed, gate_part).astype(low)
    d_gated = nt(cotan, out_full)
    starts = [entering]
    for c in range(spans - 1):
        starts.append(decay[:, c] * starts[-1] + update[:, c])
    starts = jnp.stack(starts, axis=1).reshape(blocks, NSTATE, INNER)
    gated, d_gate_raw, d_mixed, d_start, d_inter, gate_sums = call(
        gate_kernel,
        grid,
        [
            ("row", partial), ("row", pre), ("row", cumul), ("span", starts), ("row", gate_raw),
            ("row", d_gated), ("all", gain), ("all", fold),
        ],
        [
            ("row", (count, INNER), low), ("row", (count, INNER), low),
            ("row", (count, INNER), f32), state_shape, square, ("all", (8, INNER), f32),
        ],
        flops=blocks * 200_000_000,
    )
    d_start = d_start.reshape(seqs, spans, NSTATE, INNER)
    lead = d_start[:, spans - 1]
    for c in range(spans - 2, -1, -1):
        lead = d_start[:, c] + decay[:, c] * lead
    arriving = carried_in(total_decay[:, 0], lead, True)
    out_grad = tn(gated, cotan)
    block_output = (stream + nn(gated, out_full)).astype(low)
    gate_grad = tn(normed, d_gate_raw)
    d_values, d_step, d_cumul, d_bc = call(
        local_kernel,
        grid,
        [
            ("row", pre), ("row", cumul), ("row", cumul_t), ("row", step), ("row", step_t),
            ("row", d_mixed), ("all", skip_row),
        ],
        [("row", (count, INNER), f32), square, square, ("row", (count, 2 * NSTATE), f32)],
        [(SPAN, SPAN)],
        flops=blocks * 500_000_000,
    )
    after = [arriving]
    for c in range(spans - 1, 0, -1):
        after.append(d_start[:, c] + decay[:, c] * after[-1])
    after = jnp.stack(after[::-1], axis=1).reshape(blocks, NSTATE, INNER)
    d_conv_in, d_step_pre, back_rows, conv_sums, head_sums = call(
        finish_kernel,
        grid,
        [
            ("row", pre), ("row", cumul), ("row", step), ("row", sigma), ("row", d_mixed),
            ("span", starts), ("span", after), ("row", d_values), ("row", d_step),
            ("row", d_cumul), ("row", d_inter), ("row", d_bc), ("row", cs), ("span", halo),
            ("all", taps), ("all", head_rows), ("all", fold),
        ],
        [
            ("row", (count, XBC), f32), square, ("seq", (seqs, 8, XBC), f32),
            ("all", (8, XBC), f32), ("all", (8, SPAN), f32),
        ],
        [(SPAN + 8, XBC), (SPAN + 8, XBC), (16, XBC)],
        backwards=True,
        flops=blocks * 200_000_000,
    )
    heads = jnp.concatenate(
        [
            head_sums[0, :HEADS],
            jnp.sum(gate_sums[1].reshape(HEADS, HEADDIM), axis=1),
            head_sums[1, :HEADS],
        ]
    )
    heads = jnp.pad(heads, (0, 8 * SPAN - 3 * HEADS)).reshape(8, SPAN)
    back_edge = passed_along(back_rows[:, : CONV - 1], "ctx", -1)
    d_conv_in = d_conv_in.reshape(seqs, length, XBC) + jnp.pad(
        back_edge, ((0, 0), (length - CONV + 1, 0), (0, 0))
    )
    d_cs = jnp.concatenate([d_conv_in.reshape(count, XBC), d_step_pre], axis=1).astype(low)
    d_normed = nt(d_cs, conv_part) + nt(d_gate_raw, gate_part)
    norm_grad = jnp.sum(d_normed * stream * inv_rms, axis=0)
    d_hat = d_normed * norm_row
    d_stream = inv_rms * d_hat - stream * inv_rms**3 * jnp.mean(
        d_hat * stream, axis=-1, keepdims=True
    )
    input_grad = (cotan.astype(f32) + d_stream).astype(low)
    members = (
        norm_grad.reshape(owners, -1),
        jnp.swapaxes(conv_sums[:CONV].reshape(CONV, owners, -1), 0, 1).reshape(owners, -1),
        conv_sums[CONV].reshape(owners, -1),
        gate_sums[0].reshape(owners, -1),
    )
    rows = width // owners
    small = packed(members, rows)
    out_grad = out_grad.reshape(owners, 2, rows, width)
    grads = jnp.concatenate(
        [
            tn(normed, d_cs)[:, : WIDE - SPARE].reshape(owners, rows, -1),
            small.reshape(owners, rows, SPARE),
            gate_grad.reshape(owners, rows, INNER),
            out_grad[:, 0],
            out_grad[:, 1],
        ],
        axis=2,
    )
    grads = jnp.pad(grads, ((0, 0), (0, 0), (0, COLUMNS - grads.shape[2])))
    owned, heads = merged(grads, heads)
    heads = heads.reshape(-1)[: 3 * HEADS].reshape(3, HEADS)
    conv_grad = owned[:, :WIDE]
    gate_grad = owned[:, WIDE : WIDE + INNER]
    begin = WIDE + INNER
    out_part = jnp.concatenate(
        [owned[:, begin : begin + width], owned[:, begin + width : begin + 2 * width]], axis=0
    )
    spare = conv_grad[:, WIDE - SPARE :].reshape(-1)
    cut = 0
    fields = []
    for member in members:
        fields.append(spare[cut : cut + member.shape[1]])
        cut += member.shape[1]
    return (
        block_output.reshape(seqs, length, width),
        input_grad.reshape(seqs, length, width),
        fields[0],
        jnp.concatenate([gate_grad, conv_grad[:, : WIDE - SPARE]], axis=1),
        fields[1].reshape(CONV, -1),
        fields[2],
        heads[0],
        heads[1],
        heads[2],
        fields[3],
        out_part,
    )


def solution(mesh):
    return jax.shard_map(
        on_device,
        mesh=mesh,
        in_specs=(
            P("dp", "ctx", None),
            P("dp"),
            P("dp", None),
            P(None, "dp"),
            P("dp"),
            P(),
            P(),
            P(),
            P("dp"),
            P("dp", None),
            P("dp", "ctx", None),
        ),
        out_specs=(
            P("dp", "ctx", None),
            P("dp", "ctx", None),
            P("dp"),
            P("dp", None),
            P(None, "dp"),
            P("dp"),
            P(),
            P(),
            P(),
            P("dp"),
            P("dp", None),
        ),
        check_vma=False,
    )
```

```python
import jax
import jax.numpy as jnp
from jax import lax
from jax.experimental import pallas as pl
from jax.experimental.pallas import tpu as pltpu
from jax.sharding import PartitionSpec as P

HEADS = 24
HEADDIM = 64
NSTATE = 128
CONV = 4
SPAN = 128
INNER = 1536
XBC = 1792
WIDE = 1920
SPARE = 104
PAIRS = HEADS // 2
TAIL_ROWS = 16

epsilon = 1e-05
low = jnp.bfloat16
f32 = jnp.float32


def nn(a, b, precision=None):
    return lax.dot_general(
        a, b, (((1,), (0,)), ((), ())), precision=precision, preferred_element_type=f32
    )


def nt(a, b):
    return lax.dot_general(a, b, (((1,), (1,)), ((), ())), preferred_element_type=f32)


def tn(a, b):
    return lax.dot_general(a, b, (((0,), (0,)), ((), ())), preferred_element_type=f32)


def silu_grad(pre):
    sigma = jax.nn.sigmoid(pre)
    return sigma * (1.0 + pre * (1.0 - sigma))


def first_half(rows):
    return lax.broadcasted_iota(jnp.int32, (rows, SPAN), 1) < HEADDIM


def expand(per_head):
    rows = per_head.shape[0]
    mask = first_half(rows)
    pieces = []
    for pair in range(PAIRS):
        left = jnp.broadcast_to(per_head[:, 2 * pair : 2 * pair + 1], (rows, SPAN))
        right = jnp.broadcast_to(per_head[:, 2 * pair + 1 : 2 * pair + 2], (rows, SPAN))
        pieces.append(jnp.where(mask, left, right))
    return jnp.concatenate(pieces, axis=1)


def head_sum(wide, fold):
    high = wide.astype(low)
    rest = (wide - high.astype(f32)).astype(low)
    return nn(high, fold) + nn(rest, fold)


def diagonal(block, mask):
    zero = jnp.zeros_like(block)
    return jnp.concatenate(
        [jnp.where(mask, block, zero), jnp.where(mask, zero, block)], axis=0
    ).astype(low)


def causal_mask():
    row = lax.broadcasted_iota(jnp.int32, (SPAN, SPAN), 0)
    column = lax.broadcasted_iota(jnp.int32, (SPAN, SPAN), 1)
    return row >= column


def decay_of(cumul, cumul_t, head, causal):
    gap = cumul[:, head : head + 1] - cumul_t[head : head + 1, :]
    return jnp.exp(jnp.where(causal, gap, -1e30))


def prepare_kernel(
    cs_ref, halo_ref, taps_ref, bias_ref, head_ref,
    pre_ref, cumul_ref, cumul_t_ref, step_ref, step_t_ref, sigma_ref, update_ref, decay_ref,
    padded,
):
    padded[0:8, :] = halo_ref[0]
    padded[8:, :] = cs_ref[:, :XBC].astype(f32)
    pre = bias_ref[...] + sum(
        padded[5 + k : 5 + k + SPAN, :] * taps_ref[k : k + 1, :] for k in range(CONV)
    )
    pre_ref[...] = pre
    active = pre * jax.nn.sigmoid(pre)
    values = active[:, :INNER]
    inputs_b = active[:, INNER : INNER + NSTATE].astype(low)
    lane = lax.broadcasted_iota(jnp.int32, (SPAN, SPAN), 1)
    raw = jnp.where(lane < HEADS, cs_ref[:, XBC:].astype(f32) + head_ref[0:1, :], 0.0)
    step = jnp.maximum(raw, 0.0) + jnp.log1p(jnp.exp(-jnp.abs(raw)))
    step = jnp.where(lane < HEADS, step, 0.0)
    sigma_ref[...] = jax.nn.sigmoid(raw)
    log_step = step * (-jnp.exp(head_ref[1:2, :]))
    lower = causal_mask().astype(f32)
    cumul = nn(lower, log_step, lax.Precision.HIGHEST)
    cumul_ref[...] = cumul
    step_ref[...] = step
    cumul_t_ref[...] = cumul.T
    step_t_ref[...] = step.T
    last = cumul[SPAN - 1 : SPAN, :]
    tail = jnp.exp(last - cumul) * step
    update_ref[0] = tn(inputs_b, (expand(tail) * values).astype(low))
    decay_ref[0] = jnp.broadcast_to(expand(jnp.exp(last)), (8, INNER))


def intra_kernel(pre_ref, cumul_ref, cumul_t_ref, step_t_ref, skip_ref, out_ref):
    pre = pre_ref[...]
    active = pre * jax.nn.sigmoid(pre)
    inputs_b = active[:, INNER : INNER + NSTATE].astype(low)
    readout = active[:, INNER + NSTATE :].astype(low)
    scores = nt(readout, inputs_b)
    causal = causal_mask()
    mask = first_half(SPAN)
    cumul, cumul_t, step_t = cumul_ref[...], cumul_t_ref[...], step_t_ref[...]
    for pair in range(PAIRS):
        cut = slice(pair * SPAN, (pair + 1) * SPAN)
        values = active[:, cut]
        weights = [
            (scores * decay_of(cumul, cumul_t, h, causal) * step_t[h : h + 1, :]).astype(low)
            for h in (2 * pair, 2 * pair + 1)
        ]
        inner = nn(jnp.concatenate(weights, axis=1), diagonal(values, mask))
        out_ref[:, cut] = inner + skip_ref[:, cut] * values


def gate_kernel(
    partial_ref, pre_ref, cumul_ref, start_ref, gate_ref, dgated_ref, gain_ref, fold_ref,
    gated_ref, dgate_ref, dmixed_ref, dstart_ref, dcumul_ref, sums_ref,
):
    @pl.when((pl.program_id(0) == 0) & (pl.program_id(1) == 0))
    def _():
        sums_ref[...] = jnp.zeros_like(sums_ref)

    pre = pre_ref[...]
    active = pre * jax.nn.sigmoid(pre)
    values = active[:, :INNER]
    readout = active[:, INNER + NSTATE :].astype(low)
    growth = expand(jnp.exp(cumul_ref[...]))
    inter = growth * nn(readout, start_ref[0].astype(low))
    mixed = partial_ref[...] + inter
    gate = gate_ref[...].astype(f32)
    sigma = jax.nn.sigmoid(gate)
    act = gate * sigma
    gate_val = mixed * act
    rms = lax.rsqrt(jnp.mean(gate_val * gate_val, axis=1, keepdims=True) + epsilon)
    hat = gate_val * rms
    gain = gain_ref[...]
    gated_ref[...] = (hat * gain).astype(low)
    d_gated = dgated_ref[...]
    sums_ref[0:1, :] += jnp.sum(d_gated * hat, axis=0, keepdims=True)
    d_hat = d_gated * gain
    d_gate = rms * d_hat - hat * (rms * rms * jnp.mean(d_hat * gate_val, axis=1, keepdims=True))
    dgate_ref[...] = (d_gate * mixed * (sigma * (1.0 + gate * (1.0 - sigma)))).astype(low)
    d_mixed = d_gate * act
    dmixed_ref[...] = d_mixed
    sums_ref[1:2, :] += jnp.sum(d_mixed * values, axis=0, keepdims=True)
    dstart_ref[0] = tn(readout, (growth * d_mixed).astype(low))
    dcumul_ref[...] = head_sum(d_mixed * inter, fold_ref[...])


def local_kernel(
    pre_ref, cumul_ref, cumul_t_ref, step_ref, step_t_ref, dmixed_ref, skip_ref,
    dvalues_ref, dstep_ref, dcumul_ref, dbc_ref, rows,
):
    pre = pre_ref[...]
    active = pre * jax.nn.sigmoid(pre)
    inputs_b = active[:, INNER : INNER + NSTATE].astype(low)
    readout = active[:, INNER + NSTATE :].astype(low)
    scores = nt(readout, inputs_b)
    causal = causal_mask()
    mask = first_half(SPAN)
    lane = lax.broadcasted_iota(jnp.int32, (SPAN, SPAN), 1)
    cumul, cumul_t, step_t = cumul_ref[...], cumul_t_ref[...], step_t_ref[...]
    rows[...] = jnp.zeros_like(rows)
    columns = jnp.zeros((SPAN, SPAN), f32)
    d_scores = jnp.zeros((SPAN, SPAN), f32)
    for pair in range(PAIRS):
        cut = slice(pair * SPAN, (pair + 1) * SPAN)
        values = active[:, cut]
        d_mixed = dmixed_ref[:, cut]
        d_low = d_mixed.astype(low)
        d_weights = nt(d_low, diagonal(values, mask))
        weights = []
        for half in range(2):
            h = 2 * pair + half
            decay = decay_of(cumul, cumul_t, h, causal)
            step_row = step_t[h : h + 1, :]
            part = d_weights[:, half * SPAN : (half + 1) * SPAN] * decay
            d_scores = d_scores + part * step_row
            scored = part * scores
            rows[h : h + 1, :] = jnp.sum(scored, axis=0, keepdims=True)
            along = jnp.sum(scored * step_row, axis=1, keepdims=True)
            columns = jnp.where(lane == h, along, columns)
            weights.append((scores * decay * step_row).astype(low))
        back = tn(jnp.concatenate(weights, axis=1), d_low)
        dvalues_ref[:, cut] = (
            jnp.where(mask, back[:SPAN], back[SPAN:]) + skip_ref[:, cut] * d_mixed
        )
    d_step = rows[...].T
    dstep_ref[...] = d_step
    dcumul_ref[...] = columns - d_step * step_ref[...]
    d_low = d_scores.astype(low)
    dbc_ref[:, :NSTATE] = tn(d_low, readout)
    dbc_ref[:, NSTATE:] = nn(d_low, inputs_b)


def finish_kernel(
    pre_ref, cumul_ref, step_ref, sigma_ref, dmixed_ref, start_ref, after_ref,
    dvalues_ref, dstep_ref, dcumul_ref, dinter_ref, dbc_ref, cs_ref, halo_ref, taps_ref,
    head_ref, fold_ref,
    dconv_ref, dpre_ref, edge_ref, sums_ref, heads_ref,
    padded, shifted, lead,
):
    first = pl.program_id(1) == 0

    @pl.when(first & (pl.program_id(0) == 0))
    def _():
        sums_ref[...] = jnp.zeros_like(sums_ref)
        heads_ref[...] = jnp.zeros_like(heads_ref)

    pre = pre_ref[...]
    sigma = jax.nn.sigmoid(pre)
    active = pre * sigma
    values = active[:, :INNER]
    inputs_b = active[:, INNER : INNER + NSTATE].astype(low)
    cumul, step = cumul_ref[...], step_ref[...]
    after = after_ref[0]
    start = start_ref[0]
    after_low = after.astype(low)
    last = cumul[SPAN - 1 : SPAN, :]
    expo_tail = jnp.exp(last - cumul)
    tail = expo_tail * step
    tail_wide = expand(tail)
    fold = fold_ref[...]
    q = nn(inputs_b, after_low)
    d_values = dvalues_ref[...] + tail_wide * q
    d_b = dbc_ref[:, :NSTATE] + nt((tail_wide * values).astype(low), after_low)
    grown = (expand(jnp.exp(cumul)) * dmixed_ref[...]).astype(low)
    d_c = dbc_ref[:, NSTATE:] + nt(grown, start.astype(low))
    d_tail = head_sum(values * q, fold)
    tail_term = d_tail * tail
    d_step = dstep_ref[...] + d_tail * expo_tail
    d_cumul = dcumul_ref[...] + dinter_ref[...] - tail_term
    both = jnp.broadcast_to(jnp.sum(after * start, axis=0, keepdims=True), (8, INNER))
    end = jnp.exp(last) * head_sum(both, fold)[0:1, :] + jnp.sum(
        tail_term, axis=0, keepdims=True
    )
    row = lax.broadcasted_iota(jnp.int32, (SPAN, SPAN), 0)
    column = lax.broadcasted_iota(jnp.int32, (SPAN, SPAN), 1)
    upper = (row <= column).astype(f32)
    d_log = nn(upper, d_cumul, lax.Precision.HIGHEST) + end
    rate = -jnp.exp(head_ref[1:2, :])
    d_pre = (d_step + d_log * rate) * sigma_ref[...]
    d_pre = jnp.where(column < HEADS, d_pre, 0.0)
    dpre_ref[...] = d_pre
    heads_ref[0:1, :] += jnp.sum(d_log * step, axis=0, keepdims=True) * rate
    heads_ref[1:2, :] += jnp.sum(d_pre, axis=0, keepdims=True)
    d_active = jnp.concatenate([d_values, d_b, d_c], axis=1)
    d_conv = d_active * (sigma * (1.0 + pre * (1.0 - sigma)))

    @pl.when(first)
    def _():
        shifted[SPAN:, :] = jnp.zeros((8, XBC), f32)

    @pl.when(jnp.logical_not(first))
    def _():
        shifted[SPAN:, :] = shifted[0:8, :]

    shifted[0:SPAN, :] = d_conv
    padded[0:8, :] = halo_ref[0]
    padded[8:, :] = cs_ref[:, :XBC].astype(f32)
    lead[0:8, :] = jnp.zeros((8, XBC), f32)
    lead[8:, :] = d_conv[0:8, :]
    dconv_ref[...] = sum(
        taps_ref[k : k + 1, :] * shifted[3 - k : 3 - k + SPAN, :] for k in range(CONV)
    )
    edge_ref[0] = sum(taps_ref[k : k + 1, :] * lead[8 - k : 16 - k, :] for k in range(CONV))
    for k in range(CONV):
        sums_ref[k : k + 1, :] += jnp.sum(
            d_conv * padded[5 + k : 5 + k + SPAN, :], axis=0, keepdims=True
        )
    sums_ref[CONV : CONV + 1, :] += jnp.sum(d_conv, axis=0, keepdims=True)


def call(kernel, grid, operands, results, scratch=(), backwards=False, flops=0):
    seqs, spans = grid

    def spec(kind, shape):
        if kind == "all":
            return pl.BlockSpec(shape, lambda b, c: (0,) * len(shape))
        if kind == "seq":
            return pl.BlockSpec((1,) + shape[1:], lambda b, c: (b, 0, 0))

        def at(b, c):
            return b * spans + ((spans - 1 - c) if backwards else c)

        if kind == "span":
            return pl.BlockSpec((1,) + shape[1:], lambda b, c: (at(b, c), 0, 0))
        return pl.BlockSpec((SPAN,) + shape[1:], lambda b, c: (at(b, c), 0))

    arrays = [array for _, array in operands]
    moved = sum(a.size * a.dtype.itemsize for a in arrays)
    return pl.pallas_call(
        kernel,
        grid=grid,
        in_specs=[spec(kind, array.shape) for kind, array in operands],
        out_specs=[spec(kind, shape) for kind, shape, _ in results],
        out_shape=[jax.ShapeDtypeStruct(shape, kept) for _, shape, kept in results],
        scratch_shapes=[pltpu.VMEM(shape, f32) for shape in scratch],
        compiler_params=pltpu.CompilerParams(vmem_limit_bytes=50 * 1024 * 1024),
        cost_estimate=pl.CostEstimate(
            flops=flops, bytes_accessed=2 * moved, transcendentals=0
        ),
    )(*arrays)


def passed_along(block, axis, distance):
    devices = range(lax.axis_size(axis))
    route = [(i - distance, i) for i in devices if i - distance in devices]
    return lax.ppermute(block, axis, route)


def carried_in(decay, state, reverse):
    count = lax.axis_size("ctx")
    place = lax.axis_index("ctx")
    high = lax.reduce_precision(decay, 8, 7)
    extra = jnp.stack([high, decay - high], axis=1)
    sent = jnp.concatenate([state, extra], axis=1).astype(low)
    sent = jnp.pad(sent, ((0, 0), (0, TAIL_ROWS - 2), (0, 0)))
    gathered = lax.all_gather(sent, "ctx")
    entering = jnp.zeros(state.shape, f32)
    for lap in range(count - 1):
        source = count - 1 - lap if reverse else lap
        member = gathered[source].astype(f32)
        scale = member[:, NSTATE : NSTATE + 1] + member[:, NSTATE + 1 : NSTATE + 2]
        passed = scale * entering + member[:, :NSTATE]
        wanted = source > place if reverse else source < place
        entering = jnp.where(wanted, passed, entering)
    return entering


COLUMNS = 5120
MESH = pl.DeviceIdType.MESH


def power(size):
    return size.bit_length() - 1


def orders():
    ctx = [("ctx", bit) for bit in range(power(lax.axis_size("ctx")))]
    own = [("dp", bit) for bit in range(power(lax.axis_size("dp")))]
    return (
        ctx + own[1:2] + own[:1] + own[2:],
        ctx[:1] + own[:1] + ctx[1:] + own[1:],
    )


def bit_of(axis, bit):
    return lax.axis_index(axis) // 2**bit % 2


def partner(axis, bit):
    dp, ctx = lax.axis_index("dp"), lax.axis_index("ctx")
    move = 2**bit * (1 - 2 * bit_of(axis, bit))
    return (dp + move, ctx) if axis == "dp" else (dp, ctx + move)


def greet(steps):
    barrier = pltpu.get_barrier_semaphore()
    for axis, bit in steps:
        pl.semaphore_signal(
            barrier, inc=1, device_id=partner(axis, bit), device_id_type=MESH
        )
    pl.semaphore_wait(barrier, len(steps))


def remote(source, target, sends, receives, slot, axis, bit):
    return pltpu.make_async_remote_copy(
        src_ref=source,
        dst_ref=target,
        send_sem=sends.at[slot],
        recv_sem=receives.at[slot],
        device_id=partner(axis, bit),
        device_id_type=MESH,
    )


def region(plan, done, rows, stream, width):
    owners = []
    for bit in reversed(range(power(lax.axis_size("dp")))):
        settled = ("dp", bit) in done
        owners.append(pl.ds(bit_of("dp", bit), 1) if settled else pl.ds(0, 2))
    begin, size = 0, width
    for axis, bit in plan:
        if axis == "ctx" and (axis, bit) in done:
            size = size // 2
            begin = begin + bit_of(axis, bit) * size
    begin = pl.multiple_of(stream * width + begin, SPAN)
    return tuple(owners) + (rows, pl.ds(begin, size))


def spread_kernel(plans, shard, out, local, sends, receives):
    count = len(plans[0])
    rows, columns = shard.shape
    width = columns // 2
    every = pl.ds(0, rows)
    ones = (0,) * power(lax.axis_size("dp"))
    places = []
    for stream, plan in enumerate(plans):
        whole = region(plan, plan, every, stream, width)
        place = pltpu.make_async_copy(
            shard.at[whole[-2:]],
            out.at[tuple(bit_of("dp", bit) for bit in reversed(range(len(ones)))) + whole[-2:]],
            local.at[stream],
        )
        place.start()
        places.append(place)
    greet(plans[0])
    copies = [[], []]

    def launch(stream, step):
        plan = plans[stream]
        axis, bit = plan[count - 1 - step]
        part = out.at[region(plan, plan[: count - step], every, stream, width)]
        copy = remote(part, part, sends, receives, stream * count + step, axis, bit)
        copy.start()
        copies[stream].append(copy)

    for stream in range(2):
        places[stream].wait()
        launch(stream, 0)
    for step in range(count):
        for stream in range(2):
            copies[stream][step].wait_recv()
            if step < count - 1:
                launch(stream, step + 1)
    for stream in range(2):
        for copy in copies[stream]:
            copy.wait_send()


def merge_kernel(
    plans, deep, cs_ref, gate_ref, out_ref, heads_ref, total_ref, heads_out,
    whole, sums, final, head_sums, head_arrived,
    local, sends, receives, last_sends, last_receives, head_sends, head_receives, *arrived,
):
    count = len(plans[0])
    rows, columns = whole.shape[-2:]
    width = columns // 2
    every = pl.ds(0, rows)
    lead = (slice(None),) * (len(whole.shape) - 2)
    begin = WIDE + INNER
    span = out_ref.shape[-1]
    places = []
    for source, at in (
        (cs_ref, 0), (gate_ref, WIDE),
        (out_ref.at[lead + (0,)], begin), (out_ref.at[lead + (1,)], begin + span),
    ):
        place = pltpu.make_async_copy(
            source,
            whole.at[lead + (every, pl.ds(at, source.shape[-1]))],
            local.at[len(places)],
        )
        place.start()
        places.append(place)
    rest = begin + 2 * span
    if rest < columns:
        whole[lead + (every, pl.ds(rest, columns - rest))] = jnp.zeros(
            whole.shape[:-1] + (columns - rest,), low
        )
    greet(plans[0])
    copies = [[], []]
    head_copies = []
    head_sums[0] = heads_ref[...]

    def launch(stream, step):
        plan = plans[stream]
        axis, bit = plan[step]
        part = list(region(plan, plan[:step], every, stream, width))
        move = 1 - bit_of(axis, bit)
        if axis == "dp":
            part[power(lax.axis_size("dp")) - 1 - bit] = pl.ds(move, 1)
        else:
            size = part[-1].size // 2
            part[-1] = pl.ds(pl.multiple_of(part[-1].start + move * size, SPAN), size)
        held = whole if step == 0 else sums
        copy = remote(
            held.at[tuple(part)], arrived[stream * count + step],
            sends, receives, stream * count + step, axis, bit,
        )
        copy.start()
        copies[stream].append(copy)

    def launch_heads(step):
        axis, bit = plans[0][step]
        copy = remote(
            head_sums.at[step], head_arrived.at[step], head_sends, head_receives, step, axis, bit
        )
        copy.start()
        head_copies.append(copy)

    launch_heads(0)
    for place in places:
        place.wait()
    for stream in range(2):
        launch(stream, 0)
    for step in range(count):
        for stream in range(2):
            plan = plans[stream]
            copies[stream][step].wait_recv()
            held = whole if step == 0 else sums
            came = arrived[stream * count + step]

            def add(index, carry, held=held, came=came, plan=plan, stream=stream, step=step):
                some = pl.ds(pl.multiple_of(index * 16, 16), 16)
                part = region(plan, plan[: step + 1], some, stream, width)
                other = lead + (some, slice(None))
                sums[part] = (held[part].astype(f32) + came[other].astype(f32)).astype(low)
                return carry

            lax.fori_loop(0, rows // 16, add, 0)
            if step < count - 1:
                launch(stream, step + 1)
        head_copies[step].wait_recv()
        head_sums[step + 1] = head_sums[step] + head_arrived[step]
        if step < count - 1:
            launch_heads(step + 1)
    heads_out[...] = head_sums[count]
    last = [[], []]
    for stream, plan in enumerate(plans):
        mine = region(plan, plan, every, stream, width)
        size = mine[-1].size
        final[mine[-2:]] = sums[mine].reshape(rows, size)
    for step in range(deep):
        for stream, plan in enumerate(plans):
            ctx = [member for member in plan if member[0] == "ctx"]
            axis, bit = ctx[deep - 1 - step]
            part = final.at[region(plan, ctx[: deep - step], every, stream, width)[-2:]]
            copy = remote(
                part, part, last_sends, last_receives, stream * deep + step, axis, bit
            )
            copy.start()
            last[stream].append(copy)
        for stream in range(2):
            last[stream][step].wait_recv()
    total_ref[...] = final[...].astype(f32)
    for stream in range(2):
        for copy in copies[stream] + last[stream]:
            copy.wait_send()
    for copy in head_copies:
        copy.wait_send()


def padded_rows(rows):
    return -(-rows // 16) * 16


def spread(shard):
    rows = shard.shape[0]
    full = padded_rows(rows)
    owners = lax.axis_size("dp")
    plans = orders()
    count = len(plans[0])
    any_spec = pl.BlockSpec(memory_space=pl.ANY)
    split = (2,) * power(owners)
    result = pl.pallas_call(
        lambda *refs: spread_kernel(plans, *refs),
        out_shape=jax.ShapeDtypeStruct(split + (full, COLUMNS), shard.dtype),
        in_specs=[any_spec],
        out_specs=any_spec,
        scratch_shapes=[
            pltpu.SemaphoreType.DMA((2,)),
            pltpu.SemaphoreType.DMA((2 * count,)),
            pltpu.SemaphoreType.DMA((2 * count,)),
        ],
        compiler_params=pltpu.CompilerParams(collective_id=0, has_side_effects=True),
    )(jnp.pad(shard, ((0, full - rows), (0, 0))))
    return result.reshape(owners, full, COLUMNS)[:, :rows]


def merged(cs_grad, gate_grad, out_grad, heads):
    owners = lax.axis_size("dp")
    rows = cs_grad.shape[0] // owners
    full = padded_rows(rows)
    plans = orders()
    count, deep = len(plans[0]), power(lax.axis_size("ctx"))
    split = (2,) * power(owners)

    def owned(grad, parts):
        shape = (owners,) + parts + (rows, grad.shape[-1])
        fill = ((0, 0),) * (1 + len(parts)) + ((0, full - rows), (0, 0))
        wide = jnp.pad(grad.reshape(shape), fill)
        return wide.reshape(split + parts + (full, grad.shape[-1]))

    halves = []
    for plan in plans:
        sizes, width = [2] * len(split), COLUMNS // 2
        for axis, bit in plan:
            if axis == "dp":
                sizes[len(split) - 1 - bit] = 1
            else:
                width //= 2
            halves.append(pltpu.VMEM(tuple(sizes) + (full, width), low))
    vmem = pl.BlockSpec(memory_space=pltpu.VMEM)
    any_spec = pl.BlockSpec(memory_space=pl.ANY)
    dma = pltpu.SemaphoreType.DMA
    total, heads = pl.pallas_call(
        lambda *refs: merge_kernel(plans, deep, *refs),
        out_shape=[
            jax.ShapeDtypeStruct((full, COLUMNS), f32), jax.ShapeDtypeStruct(heads.shape, f32)
        ],
        in_specs=[any_spec] * 3 + [vmem],
        out_specs=[vmem] * 2,
        scratch_shapes=[
            pltpu.VMEM(split + (full, COLUMNS), low),
            pltpu.VMEM(split + (full, COLUMNS), low),
            pltpu.VMEM((full, COLUMNS), low),
            pltpu.VMEM((count + 1,) + heads.shape, f32),
            pltpu.VMEM((count,) + heads.shape, f32),
            dma((4,)),
            dma((2 * count,)),
            dma((2 * count,)),
            dma((2 * deep,)),
            dma((2 * deep,)),
            dma((count,)),
            dma((count,)),
        ]
        + halves,
        compiler_params=pltpu.CompilerParams(
            collective_id=1, has_side_effects=True, vmem_limit_bytes=50 * 1024 * 1024
        ),
    )(owned(cs_grad, ()), owned(gate_grad, ()), owned(out_grad, (2,)), heads)
    return total[:rows], heads


def packed(parts, rows):
    flat = jnp.concatenate([part.reshape(part.shape[0], -1) for part in parts], axis=1)
    return jnp.pad(flat, ((0, 0), (0, rows * SPARE - flat.shape[1]))).reshape(-1, SPARE)


def gather_weights(norm_weight, in_weight, conv_weight, conv_bias, gated_gain, out_weight):
    rows = in_weight.shape[0]
    owners = lax.axis_size("dp")
    members = (norm_weight, conv_weight, conv_bias, gated_gain)
    small = packed([part.reshape(1, -1) for part in members], rows)
    width = out_weight.shape[1]
    shard = jnp.concatenate(
        [in_weight[:, INNER:], small, in_weight[:, :INNER], out_weight[:rows], out_weight[rows:]],
        axis=1,
    )
    whole = spread(jnp.pad(shard, ((0, 0), (0, COLUMNS - shard.shape[1]))))
    flat = whole.reshape(owners * rows, COLUMNS)
    begin = WIDE + INNER
    out_full = jnp.stack(
        [whole[:, :, begin : begin + width], whole[:, :, begin + width : begin + 2 * width]], axis=1
    ).reshape(-1, width)
    conv_part = flat[:, :WIDE]
    spare = conv_part[:, WIDE - SPARE :].reshape(owners, rows * SPARE)
    cut = 0
    fields = []
    for member in members:
        fields.append(spare[:, cut : cut + member.size])
        cut += member.size
    conv_full = jnp.swapaxes(fields[1].reshape(owners, CONV, -1), 0, 1).reshape(CONV, -1)
    return (
        fields[0].reshape(1, -1).astype(f32),
        conv_part,
        flat[:, WIDE : WIDE + INNER],
        conv_full.astype(f32),
        fields[2].reshape(1, -1).astype(f32),
        fields[3].reshape(1, -1).astype(f32),
        out_full,
    )


def on_device(
    tokens,
    norm_weight,
    in_weight,
    conv_weight,
    conv_bias,
    decay_log,
    skip_gain,
    step_bias,
    gated_gain,
    out_weight,
    cotangent,
):
    seqs, length, width = tokens.shape
    count = seqs * length
    spans = length // SPAN
    grid = (seqs, spans)
    blocks = seqs * spans
    owners = lax.axis_size("dp")
    norm_row, conv_part, gate_part, taps, bias, gain, out_full = gather_weights(
        norm_weight, in_weight, conv_weight, conv_bias, gated_gain, out_weight
    )
    stream = tokens.reshape(count, width).astype(f32)
    cotan = cotangent.reshape(count, width)
    inv_rms = lax.rsqrt(jnp.mean(stream * stream, axis=-1, keepdims=True) + epsilon)
    normed = (stream * inv_rms * norm_row).astype(low)
    cs = nn(normed, conv_part).astype(low)
    conv_in = cs[:, :XBC].reshape(seqs, spans, SPAN, XBC)
    ends = conv_in[:, :, SPAN - CONV + 1 :]
    edge = passed_along(ends[:, -1], "ctx", 1)
    halo = jnp.concatenate([edge[:, None], ends[:, :-1]], axis=1).astype(f32)
    halo = jnp.pad(halo, ((0, 0), (0, 0), (8 - CONV + 1, 0), (0, 0))).reshape(blocks, 8, XBC)
    head_rows = jnp.pad(jnp.stack([step_bias, decay_log]), ((0, 6), (0, SPAN - HEADS)))
    skip_row = jnp.repeat(skip_gain, HEADDIM)[None]
    fold = (jnp.arange(INNER)[:, None] // HEADDIM == jnp.arange(SPAN)[None]).astype(low)
    square = ("row", (count, SPAN), f32)
    state_shape = ("span", (blocks, NSTATE, INNER), f32)
    pre, cumul, cumul_t, step, step_t, sigma, update, decay = call(
        prepare_kernel,
        grid,
        [("row", cs), ("span", halo), ("all", taps), ("all", bias), ("all", head_rows)],
        [("row", (count, XBC), f32)] + [square] * 5 + [state_shape, ("span", (blocks, 8, INNER), f32)],
        [(SPAN + 8, XBC)],
        flops=blocks * 60_000_000,
    )
    decay = decay[:, :1].reshape(seqs, spans, 1, INNER)
    update = update.reshape(seqs, spans, NSTATE, INNER)
    total, total_decay = update[:, 0], decay[:, 0]
    for c in range(1, spans):
        total = decay[:, c] * total + update[:, c]
        total_decay = total_decay * decay[:, c]
    entering = carried_in(total_decay[:, 0], total, False)
    partial, = call(
        intra_kernel,
        grid,
        [("row", pre), ("row", cumul), ("row", cumul_t), ("row", step_t), ("all", skip_row)],
        [("row", (count, INNER), f32)],
        flops=blocks * 300_000_000,
    )
    gate_raw = nn(normed, gate_part).astype(low)
    d_gated = nt(cotan, out_full)
    starts = [entering]
    for c in range(spans - 1):
        starts.append(decay[:, c] * starts[-1] + update[:, c])
    starts = jnp.stack(starts, axis=1).reshape(blocks, NSTATE, INNER)
    gated, d_gate_raw, d_mixed, d_start, d_inter, gate_sums = call(
        gate_kernel,
        grid,
        [
            ("row", partial), ("row", pre), ("row", cumul), ("span", starts), ("row", gate_raw),
            ("row", d_gated), ("all", gain), ("all", fold),
        ],
        [
            ("row", (count, INNER), low), ("row", (count, INNER), low),
            ("row", (count, INNER), f32), state_shape, square, ("all", (8, INNER), f32),
        ],
        flops=blocks * 200_000_000,
    )
    d_start = d_start.reshape(seqs, spans, NSTATE, INNER)
    lead = d_start[:, spans - 1]
    for c in range(spans - 2, -1, -1):
        lead = d_start[:, c] + decay[:, c] * lead
    arriving = carried_in(total_decay[:, 0], lead, True)
    out_grad = tn(gated, cotan)
    block_output = (stream + nn(gated, out_full)).astype(low)
    gate_grad = tn(normed, d_gate_raw).astype(low)
    d_values, d_step, d_cumul, d_bc = call(
        local_kernel,
        grid,
        [
            ("row", pre), ("row", cumul), ("row", cumul_t), ("row", step), ("row", step_t),
            ("row", d_mixed), ("all", skip_row),
        ],
        [("row", (count, INNER), f32), square, square, ("row", (count, 2 * NSTATE), f32)],
        [(SPAN, SPAN)],
        flops=blocks * 500_000_000,
    )
    after = [arriving]
    for c in range(spans - 1, 0, -1):
        after.append(d_start[:, c] + decay[:, c] * after[-1])
    after = jnp.stack(after[::-1], axis=1).reshape(blocks, NSTATE, INNER)
    d_conv_in, d_step_pre, back_rows, conv_sums, head_sums = call(
        finish_kernel,
        grid,
        [
            ("row", pre), ("row", cumul), ("row", step), ("row", sigma), ("row", d_mixed),
            ("span", starts), ("span", after), ("row", d_values), ("row", d_step),
            ("row", d_cumul), ("row", d_inter), ("row", d_bc), ("row", cs), ("span", halo),
            ("all", taps), ("all", head_rows), ("all", fold),
        ],
        [
            ("row", (count, XBC), f32), square, ("seq", (seqs, 8, XBC), f32),
            ("all", (8, XBC), f32), ("all", (8, SPAN), f32),
        ],
        [(SPAN + 8, XBC), (SPAN + 8, XBC), (16, XBC)],
        backwards=True,
        flops=blocks * 200_000_000,
    )
    heads = jnp.concatenate(
        [
            head_sums[0, :HEADS],
            jnp.sum(gate_sums[1].reshape(HEADS, HEADDIM), axis=1),
            head_sums[1, :HEADS],
        ]
    )
    heads = jnp.pad(heads, (0, 8 * SPAN - 3 * HEADS)).reshape(8, SPAN)
    back_edge = passed_along(back_rows[:, : CONV - 1], "ctx", -1)
    d_conv_in = d_conv_in.reshape(seqs, length, XBC) + jnp.pad(
        back_edge, ((0, 0), (length - CONV + 1, 0), (0, 0))
    )
    d_cs = jnp.concatenate([d_conv_in.reshape(count, XBC), d_step_pre], axis=1).astype(low)
    d_normed = nt(d_cs, conv_part) + nt(d_gate_raw, gate_part)
    norm_grad = jnp.sum(d_normed * stream * inv_rms, axis=0)
    d_hat = d_normed * norm_row
    d_stream = inv_rms * d_hat - stream * inv_rms**3 * jnp.mean(
        d_hat * stream, axis=-1, keepdims=True
    )
    input_grad = (cotan.astype(f32) + d_stream).astype(low)
    members = (
        norm_grad.reshape(owners, -1),
        jnp.swapaxes(conv_sums[:CONV].reshape(CONV, owners, -1), 0, 1).reshape(owners, -1),
        conv_sums[CONV].reshape(owners, -1),
        gate_sums[0].reshape(owners, -1),
    )
    rows = width // owners
    small = packed(members, rows)
    cs_grad = tn(normed, d_cs) + jnp.pad(small, ((0, 0), (WIDE - SPARE, 0)))
    owned, heads = merged(cs_grad.astype(low), gate_grad, out_grad.astype(low), heads)
    heads = heads.reshape(-1)[: 3 * HEADS].reshape(3, HEADS)
    conv_grad = owned[:, :WIDE]
    gate_grad = owned[:, WIDE : WIDE + INNER]
    begin = WIDE + INNER
    out_part = jnp.concatenate(
        [owned[:, begin : begin + width], owned[:, begin + width : begin + 2 * width]], axis=0
    )
    spare = conv_grad[:, WIDE - SPARE :].reshape(-1)
    cut = 0
    fields = []
    for member in members:
        fields.append(spare[cut : cut + member.shape[1]])
        cut += member.shape[1]
    return (
        block_output.reshape(seqs, length, width),
        input_grad.reshape(seqs, length, width),
        fields[0],
        jnp.concatenate([gate_grad, conv_grad[:, : WIDE - SPARE]], axis=1),
        fields[1].reshape(CONV, -1),
        fields[2],
        heads[0],
        heads[1],
        heads[2],
        fields[3],
        out_part,
    )


def solution(mesh):
    return jax.shard_map(
        on_device,
        mesh=mesh,
        in_specs=(
            P("dp", "ctx", None),
            P("dp"),
            P("dp", None),
            P(None, "dp"),
            P("dp"),
            P(),
            P(),
            P(),
            P("dp"),
            P("dp", None),
            P("dp", "ctx", None),
        ),
        out_specs=(
            P("dp", "ctx", None),
            P("dp", "ctx", None),
            P("dp"),
            P("dp", None),
            P(None, "dp"),
            P("dp"),
            P(),
            P(),
            P(),
            P("dp"),
            P("dp", None),
        ),
        check_vma=False,
    )
```
